128 devices in a mesh: expert: 8 (over z_lo, y), dp: 16 (over z_hi, x, core).
Axes of the slice: x: 4, y: 4, z: 4 (z_hi: 2, z_lo: 2; z = z_hi * 2 + z_lo), core: 2. Of those that a mesh axis runs over, the one named last changes fastest.
Arguments:
- tokens: bfloat16 [2048, 7168], P('dp', 'expert'), may hold values from -6 to 6
- grad_out: bfloat16 [2048, 7168], P('dp', 'expert'), may hold values from -6 to 6
- expert_ids: int32 [2048, 2], P('dp'), may hold values from -1 to 7, as said below
- route_weights: float32 [2048, 2], P('dp'), may hold values from 0.1 to 1
- w_gate: bfloat16 [8, 7168, 2048], P('expert', 'dp'), may hold values from -0.0625 to 0.0625
- w_up: bfloat16 [8, 7168, 2048], P('expert', 'dp'), may hold values from -0.0625 to 0.0625
- w_down: bfloat16 [8, 2048, 7168], P('expert', None, 'dp'), may hold values from -0.125 to 0.125
Outputs:
- grad_tokens: bfloat16 [2048, 7168], P('dp', 'expert')
- grad_gate: bfloat16 [8, 7168, 2048], P('expert', 'dp')
- grad_up: bfloat16 [8, 7168, 2048], P('expert', 'dp')
- grad_down: bfloat16 [8, 2048, 7168], P('expert', None, 'dp')
The draws below stay inside these ranges and needn't reach their ends.
Inputs may be any that keep to these rules, and one draw needn't show every extreme that they name: expert_ids[t, 0] is an expert; expert_ids[t, 1] is another expert or -1. Within each block of 128 rows (the tokens of one index of dp) no expert appears in more than 64 rows, and one expert, the same in every block, appears in exactly 64 rows, each of which has -1 as its second entry.
All inputs are finite; a program needn't handle non-finite values.
Results may differ from the reference program's by a relative error of at most 0.03.
Values may be sent and summed in bfloat16 or wider, within the bound.
A program may use at most 128 MiB of HBM per device.

```python
import math
import jax
import jax.numpy as jnp
from jax import lax

D = 7168
FF = 2048
TOK_DEV = 128
EXPERTS = 8
CAP = 64
TOKENS = 2048
N_DP = 16


def draw_expert_ids(key, part):
    blocks = TOKENS // TOK_DEV
    keys = jax.random.split(jax.random.fold_in(key, 11), 6)
    hottest = jax.random.randint(keys[0], (), 0, EXPERTS)
    order_keys = jax.random.split(keys[1], blocks)
    orders = jax.vmap(lambda single: jax.random.permutation(single, TOK_DEV))(order_keys)
    ranks = jnp.argsort(orders, axis=1, stable=True)
    is_hot = ranks < CAP
    first_off = jnp.minimum(jax.random.randint(keys[2], (blocks, TOK_DEV), 0, EXPERTS - 1), jax.random.randint(keys[3], (blocks, TOK_DEV), 0, EXPERTS - 1))
    first = jnp.where(is_hot, hottest, (hottest + 1 + first_off) % EXPERTS)
    second_off = jax.random.randint(keys[4], (blocks, TOK_DEV), 0, EXPERTS - 2)
    second_off = jnp.where(second_off < first_off, second_off, second_off + 1)
    second = (hottest + 1 + second_off) % EXPERTS
    use_two = (jax.random.randint(keys[5], (blocks, TOK_DEV), 0, 2) == 1) & jnp.logical_not(is_hot)
    second = jnp.where(use_two, second, -1)
    return jnp.stack([first, second], axis=-1).reshape(TOKENS, 2).astype(jnp.int32)


def shard_levels(own_key, shape, shards, least, largest):
    level = 1.0
    for axis_at, shards_of in shards:
        heights = jax.random.uniform(jax.random.fold_in(jax.random.fold_in(own_key, 6), axis_at), (shards_of,), jnp.float32, least / len(shards), largest / len(shards))
        level = level * jnp.repeat(jnp.exp(heights), shape[axis_at] // shards_of).reshape((-1,) + (1,) * (len(shape) - 1 - axis_at))
    return level


def centred(key, shape, deviation, bound, shards=(), held_as=jnp.bfloat16):
    loudness = shard_levels(key, shape, shards, -0.22, 0.18) if shards else 1.0
    entries = jax.random.normal(key, shape, jnp.float32) * deviation * loudness
    return jnp.minimum(jnp.maximum(entries, -bound), bound).astype(held_as)


def setup_inputs(seed: int = 0) -> dict:
    arg_keys = jax.random.split(jax.random.key(seed), 8)
    return {
        "tokens": centred(arg_keys[0], (TOKENS, D), 1.0, 6.0, ((0, 16), (1, 8))),
        "grad_out": centred(arg_keys[1], (TOKENS, D), 1.0, 6.0, ((0, 16), (1, 8))),
        "expert_ids": draw_expert_ids(jax.random.fold_in(arg_keys[7], 71), 0),
        "route_weights": jnp.clip(jnp.exp(math.log(1.0) - 2.3025851 * jax.random.uniform(arg_keys[3], (TOKENS, 2), jnp.float32) ** shard_levels(arg_keys[3], (TOKENS, 2), ((0, 16),), -0.2, 0.2)), 0.1, 1.0),
        "w_gate": centred(arg_keys[4], (EXPERTS, D, FF), D ** -0.5, 0.0625, ((0, 8), (1, 16))),
        "w_up": centred(arg_keys[5], (EXPERTS, D, FF), D ** -0.5, 0.0625, ((0, 8), (1, 16))),
        "w_down": centred(arg_keys[6], (EXPERTS, FF, D), FF ** -0.5, 0.125, ((0, 8), (2, 16))),
    }


def blocked_sum(rows, blocks, form):
    parts = jnp.einsum(form, rows, blocks)
    rounded = lax.optimization_barrier(parts.astype(jnp.bfloat16))
    return lax.optimization_barrier(jnp.sum(rounded.astype(jnp.float32), axis=1))

def reference(tokens, grad_out, expert_ids, route_weights, w_gate, w_up, w_down):
    slots = N_DP * CAP
    width = D // N_DP
    inv_root = 1.0 / math.sqrt(TOKENS)
    flat_ids = expert_ids.reshape(-1)
    flat_token = (jnp.arange(TOKENS * 2, dtype=jnp.int32) // 2).astype(jnp.int32)
    flat_weight = route_weights.reshape(-1)
    dx_total = jnp.zeros((TOKENS, D), jnp.float32)
    grads_gate = []
    grads_up = []
    grads_down = []
    for expert in range(EXPERTS):
        chosen = flat_ids == expert
        position = jnp.cumsum(chosen.astype(jnp.int32)) - 1
        position = jnp.where(chosen, position, slots).astype(jnp.int32)
        row_index = jnp.zeros((slots,), jnp.int32).at[position].set(flat_token, mode='drop')
        filled = jnp.zeros((slots,), jnp.float32).at[position].set(1.0, mode='drop')
        weight = jnp.zeros((slots,), jnp.float32).at[position].set(flat_weight, mode='drop')
        x_rows = jnp.where(filled[:, None] > 0, tokens[row_index], 0.0).astype(jnp.bfloat16)
        g_rows = jnp.where(filled[:, None] > 0, grad_out[row_index], 0.0).astype(jnp.bfloat16)
        x_blocks = x_rows.astype(jnp.float32).reshape(slots, N_DP, width)
        g_blocks = g_rows.astype(jnp.float32).reshape(slots, N_DP, width)
        gate = blocked_sum(x_blocks, w_gate[expert].astype(jnp.float32).reshape(N_DP, width, FF), 'sbd,bdf->sbf')
        upper = blocked_sum(x_blocks, w_up[expert].astype(jnp.float32).reshape(N_DP, width, FF), 'sbd,bdf->sbf')
        back = blocked_sum(g_blocks, w_down[expert].astype(jnp.float32).reshape(FF, N_DP, width), 'sbd,fbd->sbf')
        back = back * weight[:, None]
        sigmoid_gate = jax.nn.sigmoid(gate)
        scaled = (weight[:, None] * gate * sigmoid_gate * upper).astype(jnp.bfloat16)
        d_gate = (back * upper * sigmoid_gate * (1.0 + gate * (1.0 - sigmoid_gate))).astype(jnp.bfloat16)
        d_up = (back * gate * sigmoid_gate).astype(jnp.bfloat16)
        grads_gate.append((jnp.dot(x_rows.T, d_gate, preferred_element_type=jnp.float32) * inv_root).astype(jnp.bfloat16))
        grads_up.append((jnp.dot(x_rows.T, d_up, preferred_element_type=jnp.float32) * inv_root).astype(jnp.bfloat16))
        grads_down.append((jnp.dot(scaled.T, g_rows, preferred_element_type=jnp.float32) * inv_root).astype(jnp.bfloat16))
        part = (jnp.dot(d_gate, w_gate[expert].T, preferred_element_type=jnp.float32) + jnp.dot(d_up, w_up[expert].T, preferred_element_type=jnp.float32)).astype(jnp.bfloat16)
        dx_total = dx_total.at[row_index].add(jnp.where(filled[:, None] > 0, part.astype(jnp.float32), 0.0))
    return (dx_total.astype(jnp.bfloat16), jnp.stack(grads_gate), jnp.stack(grads_up), jnp.stack(grads_down))
```

```python
import math

import jax
import jax.numpy as jnp
from jax import lax
from jax.sharding import PartitionSpec as P


def body(tokens, grad_out, expert_ids, route_weights, w_gate, w_up, w_down):
    experts = lax.axis_size("expert")
    groups = lax.axis_size("dp")
    tok_rows, width = tokens.shape
    capacity = tok_rows // 2
    hidden = w_gate.shape[2]
    slots = groups * capacity
    expert_index = lax.axis_index("expert")
    inv_root = 1.0 / math.sqrt(tok_rows * groups)
    rows_first = (((0,), (0,)), ((), ()))
    last_dims = (((1,), (1,)), ((), ()))
    gate_shard, up_shard, down_shard = w_gate[0], w_up[0], w_down[0]
    shard = gate_shard.shape[0]
    halves = width // shard

    names = jnp.arange(experts, dtype=jnp.int32)[:, None]
    hit0 = expert_ids[:, 0][None, :] == names
    hit1 = expert_ids[:, 1][None, :] == names
    hit = (hit0 | hit1).astype(jnp.bfloat16)
    index = jnp.arange(tok_rows, dtype=jnp.int32)
    before = (index[:, None] < index[None, :]).astype(jnp.bfloat16)
    rank = jnp.dot(hit, before, preferred_element_type=jnp.float32)
    rank = jnp.where(hit > 0, rank, -1.0).astype(jnp.int32)
    chosen = rank[:, None, :] == jnp.arange(capacity, dtype=jnp.int32)[None, :, None]
    dispatch = chosen.astype(jnp.bfloat16).reshape(experts * capacity, tok_rows)
    weight_of = jnp.where(hit0, route_weights[:, 0][None, :], 0.0) + jnp.where(
        hit1, route_weights[:, 1][None, :], 0.0
    )
    own_rank = lax.dynamic_slice_in_dim(rank, expert_index, 1)
    own_weight_of = lax.dynamic_slice_in_dim(weight_of, expert_index, 1)
    own_weight = jnp.sum(
        jnp.where(
            own_rank == jnp.arange(capacity, dtype=jnp.int32)[:, None], own_weight_of, 0.0
        ),
        axis=1,
    )

    def send(rows):
        picked = [
            jnp.dot(
                dispatch,
                rows[:, h * shard : (h + 1) * shard],
                preferred_element_type=jnp.float32,
            )
            .astype(jnp.bfloat16)
            .reshape(experts, 1, capacity, shard)
            for h in range(halves)
        ]
        moved = lax.all_to_all(
            jnp.concatenate(picked, axis=1), "expert", split_axis=0, concat_axis=0, tiled=True
        )
        return lax.all_to_all(
            moved.reshape(groups, capacity, shard), "dp", split_axis=0, concat_axis=0, tiled=True
        ).reshape(slots, shard)

    x_block = send(tokens)
    g_block = send(grad_out)
    gate = jnp.dot(x_block, gate_shard, preferred_element_type=jnp.float32)
    upper = jnp.dot(x_block, up_shard, preferred_element_type=jnp.float32)
    back = lax.dot_general(g_block, down_shard, last_dims, preferred_element_type=jnp.float32)
    mine = lax.psum_scatter(
        jnp.concatenate([gate, upper, back], axis=1).astype(jnp.bfloat16),
        "dp",
        scatter_dimension=0,
        tiled=True,
    ).astype(jnp.float32)
    gate = mine[:, :hidden]
    upper = mine[:, hidden : 2 * hidden]
    back = mine[:, 2 * hidden :] * own_weight[:, None]
    sigmoid_gate = jax.nn.sigmoid(gate)
    scaled = own_weight[:, None] * gate * sigmoid_gate * upper
    d_gate = back * upper * sigmoid_gate * (1.0 + gate * (1.0 - sigmoid_gate))
    d_up = back * gate * sigmoid_gate
    local = jnp.concatenate([scaled, d_gate, d_up], axis=1).astype(jnp.bfloat16)
    piece = lax.all_gather(local, "dp", axis=0, tiled=True)
    scaled = piece[:, :hidden]
    d_gate = piece[:, hidden : 2 * hidden]
    d_up = piece[:, 2 * hidden :]
    block_dx = lax.dot_general(
        d_gate, gate_shard, last_dims, preferred_element_type=jnp.float32
    ) + lax.dot_general(d_up, up_shard, last_dims, preferred_element_type=jnp.float32)
    dx_rows = block_dx.astype(jnp.bfloat16)
    returned = lax.all_to_all(
        dx_rows.reshape(groups, capacity, shard), "dp", split_axis=0, concat_axis=0, tiled=True
    )
    returned = lax.all_to_all(
        returned.reshape(experts, halves, capacity, shard),
        "expert",
        split_axis=0,
        concat_axis=0,
        tiled=True,
    )
    grad_g = lax.dot_general(x_block, d_gate, rows_first, preferred_element_type=jnp.float32)
    grad_u = lax.dot_general(x_block, d_up, rows_first, preferred_element_type=jnp.float32)
    grad_d = lax.dot_general(scaled, g_block, rows_first, preferred_element_type=jnp.float32)
    grad_tokens = jnp.concatenate(
        [
            lax.dot_general(
                dispatch,
                returned[:, h].reshape(experts * capacity, shard),
                rows_first,
                preferred_element_type=jnp.float32,
            ).astype(jnp.bfloat16)
            for h in range(halves)
        ],
        axis=1,
    )
    grad_gate = (grad_g * inv_root).astype(jnp.bfloat16)[None]
    grad_up = (grad_u * inv_root).astype(jnp.bfloat16)[None]
    grad_down = (grad_d * inv_root).astype(jnp.bfloat16)[None]
    return (grad_tokens, grad_gate, grad_up, grad_down)


def solution(mesh):
    in_specs = (
        P("dp", "expert"),
        P("dp", "expert"),
        P("dp", None),
        P("dp", None),
        P("expert", "dp", None),
        P("expert", "dp", None),
        P("expert", None, "dp"),
    )
    out_specs = (
        P("dp", "expert"),
        P("expert", "dp", None),
        P("expert", "dp", None),
        P("expert", None, "dp"),
    )
    return jax.shard_map(body, mesh=mesh, in_specs=in_specs, out_specs=out_specs, check_vma=False)
```

```python
import functools
import math

import jax
import jax.numpy as jnp
from jax import lax
from jax.experimental import pallas as pl
from jax.experimental.pallas import tpu as pltpu
from jax.sharding import PartitionSpec as P

MESH = pl.DeviceIdType.MESH
CHUNKS = 8
X_WAYS, Z_WAYS, CORES = 4, 2, 2
LAST = (((1,), (1,)), ((), ()))
SUM_ORDER = "zxzzxzzx"
SPREAD_ORDER = "xzxxzxxz"


class Place:
    def __init__(self):
        self.expert = lax.axis_index("expert")
        d = lax.axis_index("dp")
        self.c = d % CORES
        self.x = (d // CORES) % X_WAYS
        self.zh = d // (CORES * X_WAYS)

    def at(self, zh, x, c):
        return (self.expert, (zh * X_WAYS + x) * CORES + c)

    def partner(self):
        return self.at(self.zh, self.x, 1 - self.c)

    def opposite(self):
        return self.at(1 - self.zh, self.x, self.c)

    def along_x(self, k):
        return (self.x + k) % X_WAYS

    def ring(self, k):
        return self.at(self.zh, self.along_x(k), self.c)

    def greet(self):
        barrier = pltpu.get_barrier_semaphore()
        peers = [self.partner(), self.opposite()] + [self.ring(k) for k in range(1, X_WAYS)]
        for peer in peers:
            pl.semaphore_signal(barrier, inc=1, device_id=peer, device_id_type=MESH)
        pl.semaphore_wait(barrier, len(peers))


def sum_kernel(
    x_ref, g_ref, wg_ref, wu_ref, wd_ref, pw_ref, out_ref,
    xp, gp, away, arrived, held, first, second, send_sem, recv_sem,
):
    me = Place()
    me.greet()
    n = wg_ref.shape[1] // CHUNKS
    blocks, rows = X_WAYS * Z_WAYS, x_ref.shape[2]

    for i in range(blocks):
        at = pl.ds(i * rows, rows)
        xp[0, at, :] = x_ref[i, me.c]
        xp[1, at, :] = x_ref[i, 1 - me.c]
        gp[0, at, :] = g_ref[i, me.c]
        gp[1, at, :] = g_ref[i, 1 - me.c]

    def copy(j, lane, src, dst, peer):
        return pltpu.make_async_remote_copy(
            src_ref=src, dst_ref=dst, send_sem=send_sem.at[j, lane], recv_sem=recv_sem.at[j, lane],
            device_id=peer, device_id_type=MESH,
        )

    def products(j, which, dst):
        cols = pl.ds(j * n, n)
        parts = (
            jnp.dot(xp[which], wg_ref[:, cols], preferred_element_type=jnp.float32),
            jnp.dot(xp[which], wu_ref[:, cols], preferred_element_type=jnp.float32),
            lax.dot_general(gp[which], wd_ref[cols, :], LAST, preferred_element_type=jnp.float32),
        )
        for k, part in enumerate(parts):
            dst[j, :, :, :, k * n : (k + 1) * n] = part.astype(jnp.bfloat16).reshape(
                Z_WAYS, X_WAYS, rows, n
            )

    def to_partner(j):
        return copy(j, 0, away.at[j], arrived.at[j], me.partner())

    def first_copies(j):
        if SUM_ORDER[j] == "x":
            return [
                copy(j, k, held.at[j, :, me.along_x(k)], first.at[j, pl.ds(2 * (k - 1), 2)], me.ring(k))
                for k in range(1, X_WAYS)
            ]
        return [copy(j, 1, held.at[j, 1 - me.zh], first.at[j, pl.ds(0, X_WAYS)], me.opposite())]

    def second_copies(j):
        if SUM_ORDER[j] == "x":
            return [copy(j, 4, held.at[j, 1 - me.zh, me.x], second.at[j, 0], me.opposite())]
        return [
            copy(j, 3 + k, held.at[j, me.zh, me.along_x(k)], second.at[j, k - 1], me.ring(k))
            for k in range(1, X_WAYS)
        ]

    f32 = jnp.float32

    def stage0(j):
        products(j, 1, away)
        to_partner(j).start()
        products(j, 0, held)

    def stage1(j):
        to_partner(j).wait_recv()
        for z in range(Z_WAYS):
            held[j, z] = (held[j, z].astype(f32) + arrived[j, z].astype(f32)).astype(jnp.bfloat16)
        for one in first_copies(j):
            one.start()

    def stage2(j):
        for one in first_copies(j):
            one.wait_recv()
        if SUM_ORDER[j] == "x":
            for z in range(Z_WAYS):
                total = held[j, z, me.x].astype(f32)
                for k in range(X_WAYS - 1):
                    total += first[j, 2 * k + z].astype(f32)
                held[j, z, me.x] = total.astype(jnp.bfloat16)
        else:
            for x in range(X_WAYS):
                held[j, me.zh, x] = (held[j, me.zh, x].astype(f32) + first[j, x].astype(f32)).astype(
                    jnp.bfloat16
                )
        for one in second_copies(j):
            one.start()

    def stage3(j):
        for one in second_copies(j):
            one.wait_recv()
        total = held[j, me.zh, me.x].astype(f32)
        for k in range(1 if SUM_ORDER[j] == "x" else X_WAYS - 1):
            total += second[j, k].astype(f32)
        weight = pw_ref[...]
        gate, upper, back = total[:, :n], total[:, n : 2 * n], total[:, 2 * n :] * weight
        s = 1.0 / (1.0 + jnp.exp(-gate))
        out_ref[j, :, :n] = (weight * gate * s * upper).astype(jnp.bfloat16)
        out_ref[j, :, n : 2 * n] = (back * upper * s * (1.0 + gate * (1.0 - s))).astype(jnp.bfloat16)
        out_ref[j, :, 2 * n :] = (back * gate * s).astype(jnp.bfloat16)

    stages = (stage0, stage1, stage2, stage3)
    lags = (0, 1, 3, 5)
    for t in range(CHUNKS + lags[-1]):
        for stage, lag in zip(stages, lags):
            if 0 <= t - lag < CHUNKS:
                stage(t - lag)
    for j in range(CHUNKS):
        for one in [to_partner(j)] + first_copies(j) + second_copies(j):
            one.wait_send()


def spread_kernel(
    inv_root, act_ref, x_ref, g_ref, wg_ref, wu_ref, gg_ref, gu_ref, gd_ref, dx_ref,
    xt, gt, whole, total, send_sem, recv_sem,
):
    me = Place()
    me.greet()
    n = wg_ref.shape[1] // CHUNKS
    blocks, rows = X_WAYS * Z_WAYS, x_ref.shape[2]
    slots = CORES * blocks * rows
    f32 = jnp.float32

    def copy(j, lane, src, dst, peer):
        return pltpu.make_async_remote_copy(
            src_ref=src, dst_ref=dst, send_sem=send_sem.at[j, lane], recv_sem=recv_sem.at[j, lane],
            device_id=peer, device_id_type=MESH,
        )

    def first_copies(j):
        if SPREAD_ORDER[j] == "x":
            return [
                copy(j, k, act_ref.at[j], whole.at[j, 0, me.zh, me.x], me.ring(k))
                for k in range(1, X_WAYS)
            ]
        return [copy(j, 1, act_ref.at[j], whole.at[j, 0, me.zh, me.x], me.opposite())]

    def second_copies(j):
        if SPREAD_ORDER[j] == "x":
            return [copy(j, 4, whole.at[j, 0, me.zh], whole.at[j, 0, me.zh], me.opposite())]
        return [
            copy(j, 3 + k, whole.at[j, 0, :, me.x], whole.at[j, 0, :, me.x], me.ring(k))
            for k in range(1, X_WAYS)
        ]

    def to_partner(j):
        return copy(j, 0, whole.at[j, 0], whole.at[j, 1], me.partner())

    def stage0(j):
        for one in first_copies(j):
            one.start()
        whole[j, 0, me.zh, me.x] = act_ref[j]

    def stage1(j):
        for one in first_copies(j):
            one.wait_recv()
        for one in second_copies(j):
            one.start()

    def stage2(j):
        for one in second_copies(j):
            one.wait_recv()
        to_partner(j).start()

    def stage3(j):
        to_partner(j).wait_recv()
        cols = pl.ds(j * n, n)
        scaled = whole[j, :, :, :, :, :n].reshape(slots, n)
        d_gate = whole[j, :, :, :, :, n : 2 * n].reshape(slots, n)
        d_up = whole[j, :, :, :, :, 2 * n :].reshape(slots, n)
        part = lax.dot_general(d_gate, wg_ref[:, cols], LAST, preferred_element_type=f32)
        part += lax.dot_general(d_up, wu_ref[:, cols], LAST, preferred_element_type=f32)
        total[...] = part if j == 0 else total[...] + part
        gg_ref[:, cols] = (jnp.dot(xt[...], d_gate, preferred_element_type=f32) * inv_root).astype(jnp.bfloat16)
        gu_ref[:, cols] = (jnp.dot(xt[...], d_up, preferred_element_type=f32) * inv_root).astype(jnp.bfloat16)
        down = jnp.dot(gt[...], scaled, preferred_element_type=f32) * inv_root
        gd_ref[cols, :] = down.T.astype(jnp.bfloat16)

    for j in range(CHUNKS):
        stage0(j)
    for i in range(blocks):
        for which in range(CORES):
            c = me.c if which == 0 else 1 - me.c
            at = pl.ds((which * blocks + i) * rows, rows)
            total[at, :] = x_ref[i, c].astype(f32)
    xt[...] = total[...].T.astype(jnp.bfloat16)
    for i in range(blocks):
        for which in range(CORES):
            c = me.c if which == 0 else 1 - me.c
            at = pl.ds((which * blocks + i) * rows, rows)
            total[at, :] = g_ref[i, c].astype(f32)
    gt[...] = total[...].T.astype(jnp.bfloat16)
    stages = (stage1, stage2, stage3)
    lags = (0, 2, 3)
    for t in range(CHUNKS + lags[-1]):
        for stage, lag in zip(stages, lags):
            if 0 <= t - lag < CHUNKS:
                stage(t - lag)
    for i in range(blocks):
        for which in range(CORES):
            c = me.c if which == 0 else 1 - me.c
            at = pl.ds((which * blocks + i) * rows, rows)
            dx_ref[i, c] = total[at, :].astype(jnp.bfloat16)
    for j in range(CHUNKS):
        for one in [to_partner(j)] + first_copies(j) + second_copies(j):
            one.wait_send()


def vmem(count):
    return [pl.BlockSpec(memory_space=pltpu.VMEM)] * count


def summed_rows(x, g, w_gate, w_up, w_down, weight):
    (blocks, cores, rows, shard), hidden = x.shape, w_gate.shape[1]
    cols = 3 * hidden // CHUNKS
    bf16 = jnp.bfloat16
    return pl.pallas_call(
        sum_kernel,
        out_shape=jax.ShapeDtypeStruct((CHUNKS, rows, cols), bf16),
        in_specs=vmem(6),
        out_specs=vmem(1)[0],
        scratch_shapes=[
            pltpu.VMEM((cores, blocks * rows, shard), bf16),
            pltpu.VMEM((cores, blocks * rows, shard), bf16),
            pltpu.VMEM((CHUNKS, Z_WAYS, X_WAYS, rows, cols), bf16),
            pltpu.VMEM((CHUNKS, Z_WAYS, X_WAYS, rows, cols), bf16),
            pltpu.VMEM((CHUNKS, Z_WAYS, X_WAYS, rows, cols), bf16),
            pltpu.VMEM((CHUNKS, 2 * (X_WAYS - 1), rows, cols), bf16),
            pltpu.VMEM((CHUNKS, X_WAYS - 1, rows, cols), bf16),
            pltpu.SemaphoreType.DMA((CHUNKS, 7)),
            pltpu.SemaphoreType.DMA((CHUNKS, 7)),
        ],
        compiler_params=pltpu.CompilerParams(
            collective_id=0, has_side_effects=True, vmem_limit_bytes=50 << 20
        ),
    )(x, g, w_gate, w_up, w_down, weight)


def spread_rows(inv_root, act, x, g, w_gate, w_up):
    (blocks, cores, rows, shard), hidden = x.shape, w_gate.shape[1]
    cols = 3 * hidden // CHUNKS
    slots = cores * blocks * rows
    bf16 = jnp.bfloat16
    return pl.pallas_call(
        functools.partial(spread_kernel, inv_root),
        out_shape=(
            jax.ShapeDtypeStruct((shard, hidden), bf16),
            jax.ShapeDtypeStruct((shard, hidden), bf16),
            jax.ShapeDtypeStruct((hidden, shard), bf16),
            jax.ShapeDtypeStruct(x.shape, bf16),
        ),
        in_specs=vmem(5),
        out_specs=vmem(4),
        scratch_shapes=[
            pltpu.VMEM((shard, slots), bf16),
            pltpu.VMEM((shard, slots), bf16),
            pltpu.VMEM((CHUNKS, cores, Z_WAYS, X_WAYS, rows, cols), bf16),
            pltpu.VMEM((slots, shard), jnp.float32),
            pltpu.SemaphoreType.DMA((CHUNKS, 7)),
            pltpu.SemaphoreType.DMA((CHUNKS, 7)),
        ],
        compiler_params=pltpu.CompilerParams(
            collective_id=1, has_side_effects=True, vmem_limit_bytes=50 << 20
        ),
    )(act, x, g, w_gate, w_up)


def body(tokens, grad_out, expert_ids, route_weights, w_gate, w_up, w_down):
    experts = lax.axis_size("expert")
    groups = lax.axis_size("dp")
    tok_rows, width = tokens.shape
    capacity = tok_rows // 2
    expert_index = lax.axis_index("expert")
    inv_root = 1.0 / math.sqrt(tok_rows * groups)
    rows_first = (((0,), (0,)), ((), ()))
    gate_shard, up_shard, down_shard = w_gate[0], w_up[0], w_down[0]
    shard = gate_shard.shape[0]
    halves = width // shard

    names = jnp.arange(experts, dtype=jnp.int32)[:, None]
    hit0 = expert_ids[:, 0][None, :] == names
    hit1 = expert_ids[:, 1][None, :] == names
    hit = (hit0 | hit1).astype(jnp.bfloat16)
    index = jnp.arange(tok_rows, dtype=jnp.int32)
    before = (index[:, None] < index[None, :]).astype(jnp.bfloat16)
    rank = jnp.dot(hit, before, preferred_element_type=jnp.float32)
    rank = jnp.where(hit > 0, rank, -1.0).astype(jnp.int32)
    chosen = rank[:, None, :] == jnp.arange(capacity, dtype=jnp.int32)[None, :, None]
    dispatch = chosen.astype(jnp.bfloat16).reshape(experts * capacity, tok_rows)
    weight_of = jnp.where(hit0, route_weights[:, 0][None, :], 0.0) + jnp.where(
        hit1, route_weights[:, 1][None, :], 0.0
    )
    own_rank = lax.dynamic_slice_in_dim(rank, expert_index, 1)
    own_weight_of = lax.dynamic_slice_in_dim(weight_of, expert_index, 1)
    own_weight = jnp.sum(
        jnp.where(
            own_rank == jnp.arange(capacity, dtype=jnp.int32)[:, None], own_weight_of, 0.0
        ),
        axis=1,
    )

    def send(rows):
        picked = [
            jnp.dot(
                dispatch,
                rows[:, h * shard : (h + 1) * shard],
                preferred_element_type=jnp.float32,
            )
            .astype(jnp.bfloat16)
            .reshape(experts, 1, capacity, shard)
            for h in range(halves)
        ]
        moved = lax.all_to_all(
            jnp.concatenate(picked, axis=1), "expert", split_axis=0, concat_axis=0, tiled=True
        )
        return lax.all_to_all(
            moved.reshape(groups, capacity, shard), "dp", split_axis=0, concat_axis=0, tiled=True
        ).reshape(groups // CORES, CORES, capacity, shard)

    x_block = send(tokens)
    g_block = send(grad_out)
    act = summed_rows(x_block, g_block, gate_shard, up_shard, down_shard, own_weight[:, None])
    grad_g, grad_u, grad_d, dx_rows = spread_rows(
        inv_root, act, x_block, g_block, gate_shard, up_shard
    )
    returned = lax.all_to_all(
        dx_rows.reshape(groups, capacity, shard), "dp", split_axis=0, concat_axis=0, tiled=True
    )
    returned = lax.all_to_all(
        returned.reshape(experts, halves, capacity, shard),
        "expert",
        split_axis=0,
        concat_axis=0,
        tiled=True,
    )
    grad_tokens = jnp.concatenate(
        [
            lax.dot_general(
                dispatch,
                returned[:, h].reshape(experts * capacity, shard),
                rows_first,
                preferred_element_type=jnp.float32,
            ).astype(jnp.bfloat16)
            for h in range(halves)
        ],
        axis=1,
    )
    return (grad_tokens, grad_g[None], grad_u[None], grad_d[None])


def solution(mesh):
    in_specs = (
        P("dp", "expert"),
        P("dp", "expert"),
        P("dp", None),
        P("dp", None),
        P("expert", "dp", None),
        P("expert", "dp", None),
        P("expert", None, "dp"),
    )
    out_specs = (
        P("dp", "expert"),
        P("expert", "dp", None),
        P("expert", "dp", None),
        P("expert", None, "dp"),
    )
    return jax.shard_map(body, mesh=mesh, in_specs=in_specs, out_specs=out_specs, check_vma=False)
```

```python
import functools
import math

import jax
import jax.numpy as jnp
from jax import lax
from jax.experimental import pallas as pl
from jax.experimental.pallas import tpu as pltpu
from jax.sharding import PartitionSpec as P

MESH = pl.DeviceIdType.MESH
CHUNKS = 8
X_WAYS, Z_WAYS, CORES = 4, 2, 2
LAST = (((1,), (1,)), ((), ()))
SUM_ORDER = "zxzzxzzx"
SPREAD_ORDER = "xzxxzxxz"


class Place:
    def __init__(self):
        self.expert = lax.axis_index("expert")
        d = lax.axis_index("dp")
        self.c = d % CORES
        self.x = (d // CORES) % X_WAYS
        self.zh = d // (CORES * X_WAYS)

    def at(self, zh, x, c):
        return (self.expert, (zh * X_WAYS + x) * CORES + c)

    def partner(self):
        return self.at(self.zh, self.x, 1 - self.c)

    def opposite(self):
        return self.at(1 - self.zh, self.x, self.c)

    def along_x(self, k):
        return (self.x + k) % X_WAYS

    def ring(self, k):
        return self.at(self.zh, self.along_x(k), self.c)

    def greet(self):
        barrier = pltpu.get_barrier_semaphore()
        peers = [self.partner(), self.opposite()] + [self.ring(k) for k in range(1, X_WAYS)]
        for peer in peers:
            pl.semaphore_signal(barrier, inc=1, device_id=peer, device_id_type=MESH)
        pl.semaphore_wait(barrier, len(peers))


def sum_kernel(
    rows_ref, wg_ref, wu_ref, wd_ref, pw_ref, out_ref,
    xp, gp, away, arrived, held, first, second, send_sem, recv_sem,
):
    me = Place()
    me.greet()
    n = wg_ref.shape[1] // CHUNKS
    blocks, rows, shard = X_WAYS * Z_WAYS, rows_ref.shape[2], wg_ref.shape[0]

    for i in range(blocks):
        at = pl.ds(i * rows, rows)
        for which in range(CORES):
            both = rows_ref[i, me.c if which == 0 else 1 - me.c]
            xp[which, at, :] = both[:, :shard]
            gp[which, at, :] = both[:, shard:]

    def copy(j, lane, src, dst, peer):
        return pltpu.make_async_remote_copy(
            src_ref=src, dst_ref=dst, send_sem=send_sem.at[j, lane], recv_sem=recv_sem.at[j, lane],
            device_id=peer, device_id_type=MESH,
        )

    def products(j, which, dst):
        cols = pl.ds(j * n, n)
        parts = (
            jnp.dot(xp[which], wg_ref[:, cols], preferred_element_type=jnp.float32),
            jnp.dot(xp[which], wu_ref[:, cols], preferred_element_type=jnp.float32),
            jnp.dot(gp[which], wd_ref[:, cols], preferred_element_type=jnp.float32),
        )
        for k, part in enumerate(parts):
            dst[j, :, :, :, k * n : (k + 1) * n] = part.astype(jnp.bfloat16).reshape(
                Z_WAYS, X_WAYS, rows, n
            )

    def to_partner(j):
        return copy(j, 0, away.at[j], arrived.at[j], me.partner())

    def first_copies(j):
        if SUM_ORDER[j] == "x":
            return [
                copy(j, k, held.at[j, :, me.along_x(k)], first.at[j, pl.ds(2 * (k - 1), 2)], me.ring(k))
                for k in range(1, X_WAYS)
            ]
        return [copy(j, 1, held.at[j, 1 - me.zh], first.at[j, pl.ds(0, X_WAYS)], me.opposite())]

    def second_copies(j):
        if SUM_ORDER[j] == "x":
            return [copy(j, 4, held.at[j, 1 - me.zh, me.x], second.at[j, 0], me.opposite())]
        return [
            copy(j, 3 + k, held.at[j, me.zh, me.along_x(k)], second.at[j, k - 1], me.ring(k))
            for k in range(1, X_WAYS)
        ]

    f32 = jnp.float32

    def stage0(j):
        products(j, 1, away)
        to_partner(j).start()
        products(j, 0, held)

    def stage1(j):
        to_partner(j).wait_recv()
        for z in range(Z_WAYS):
            held[j, z] = (held[j, z].astype(f32) + arrived[j, z].astype(f32)).astype(jnp.bfloat16)
        for one in first_copies(j):
            one.start()

    def stage2(j):
        for one in first_copies(j):
            one.wait_recv()
        if SUM_ORDER[j] == "x":
            for z in range(Z_WAYS):
                total = held[j, z, me.x].astype(f32)
                for k in range(X_WAYS - 1):
                    total += first[j, 2 * k + z].astype(f32)
                held[j, z, me.x] = total.astype(jnp.bfloat16)
        else:
            for x in range(X_WAYS):
                held[j, me.zh, x] = (held[j, me.zh, x].astype(f32) + first[j, x].astype(f32)).astype(
                    jnp.bfloat16
                )
        for one in second_copies(j):
            one.start()

    def stage3(j):
        for one in second_copies(j):
            one.wait_recv()
        total = held[j, me.zh, me.x].astype(f32)
        for k in range(1 if SUM_ORDER[j] == "x" else X_WAYS - 1):
            total += second[j, k].astype(f32)
        weight = pw_ref[...]
        gate, upper, back = total[:, :n], total[:, n : 2 * n], total[:, 2 * n :] * weight
        s = 1.0 / (1.0 + jnp.exp(-gate))
        out_ref[j, :, :n] = (weight * gate * s * upper).astype(jnp.bfloat16)
        out_ref[j, :, n : 2 * n] = (back * upper * s * (1.0 + gate * (1.0 - s))).astype(jnp.bfloat16)
        out_ref[j, :, 2 * n :] = (back * gate * s).astype(jnp.bfloat16)

    stages = (stage0, stage1, stage2, stage3)
    lags = (0, 1, 3, 5)
    for t in range(CHUNKS + lags[-1]):
        for stage, lag in zip(stages, lags):
            if 0 <= t - lag < CHUNKS:
                stage(t - lag)
    for j in range(CHUNKS):
        for one in [to_partner(j)] + first_copies(j) + second_copies(j):
            one.wait_send()


def spread_kernel(
    inv_root, act_ref, rows_ref, wg_ref, wu_ref, gg_ref, gu_ref, gd_ref, dx_ref,
    xt, gt, whole, total, send_sem, recv_sem,
):
    me = Place()
    me.greet()
    n = wg_ref.shape[1] // CHUNKS
    blocks, rows, shard = X_WAYS * Z_WAYS, rows_ref.shape[2], wg_ref.shape[0]
    slots = CORES * blocks * rows
    f32 = jnp.float32

    def copy(j, lane, src, dst, peer):
        return pltpu.make_async_remote_copy(
            src_ref=src, dst_ref=dst, send_sem=send_sem.at[j, lane], recv_sem=recv_sem.at[j, lane],
            device_id=peer, device_id_type=MESH,
        )

    def first_copies(j):
        if SPREAD_ORDER[j] == "x":
            return [
                copy(j, k, act_ref.at[j], whole.at[j, 0, me.zh, me.x], me.ring(k))
                for k in range(1, X_WAYS)
            ]
        return [copy(j, 1, act_ref.at[j], whole.at[j, 0, me.zh, me.x], me.opposite())]

    def second_copies(j):
        if SPREAD_ORDER[j] == "x":
            return [copy(j, 4, whole.at[j, 0, me.zh], whole.at[j, 0, me.zh], me.opposite())]
        return [
            copy(j, 3 + k, whole.at[j, 0, :, me.x], whole.at[j, 0, :, me.x], me.ring(k))
            for k in range(1, X_WAYS)
        ]

    def to_partner(j):
        return copy(j, 0, whole.at[j, 0], whole.at[j, 1], me.partner())

    def stage0(j):
        for one in first_copies(j):
            one.start()
        whole[j, 0, me.zh, me.x] = act_ref[j]

    def stage1(j):
        for one in first_copies(j):
            one.wait_recv()
        for one in second_copies(j):
            one.start()

    def stage2(j):
        for one in second_copies(j):
            one.wait_recv()
        to_partner(j).start()

    def stage3(j):
        to_partner(j).wait_recv()
        cols = pl.ds(j * n, n)
        scaled = whole[j, :, :, :, :, :n].reshape(slots, n)
        d_gate = whole[j, :, :, :, :, n : 2 * n].reshape(slots, n)
        d_up = whole[j, :, :, :, :, 2 * n :].reshape(slots, n)
        part = lax.dot_general(d_gate, wg_ref[:, cols], LAST, preferred_element_type=f32)
        part += lax.dot_general(d_up, wu_ref[:, cols], LAST, preferred_element_type=f32)
        total[...] = part if j == 0 else total[...] + part
        gg_ref[:, cols] = (jnp.dot(xt[...], d_gate, preferred_element_type=f32) * inv_root).astype(jnp.bfloat16)
        gu_ref[:, cols] = (jnp.dot(xt[...], d_up, preferred_element_type=f32) * inv_root).astype(jnp.bfloat16)
        gd_ref[:, cols] = (jnp.dot(gt[...], scaled, preferred_element_type=f32) * inv_root).astype(jnp.bfloat16)

    for j in range(CHUNKS):
        stage0(j)
    for lo, turned in ((0, xt), (shard, gt)):
        for i in range(blocks):
            for which in range(CORES):
                c = me.c if which == 0 else 1 - me.c
                at = pl.ds((which * blocks + i) * rows, rows)
                total[at, :] = rows_ref[i, c][:, lo : lo + shard].astype(f32)
        turned[...] = total[...].T.astype(jnp.bfloat16)
    stages = (stage1, stage2, stage3)
    lags = (0, 2, 3)
    for t in range(CHUNKS + lags[-1]):
        for stage, lag in zip(stages, lags):
            if 0 <= t - lag < CHUNKS:
                stage(t - lag)
    for i in range(blocks):
        for which in range(CORES):
            c = me.c if which == 0 else 1 - me.c
            at = pl.ds((which * blocks + i) * rows, rows)
            done = total[at, :].astype(jnp.bfloat16)
            dx_ref[i, c] = jnp.concatenate([done[: rows // 2], done[rows // 2 :]], axis=1)
    for j in range(CHUNKS):
        for one in [to_partner(j)] + first_copies(j) + second_copies(j):
            one.wait_send()


def vmem(count):
    return [pl.BlockSpec(memory_space=pltpu.VMEM)] * count


def summed_rows(packed, w_gate, w_up, w_down, weight):
    (blocks, cores, rows, _), (shard, hidden) = packed.shape, w_gate.shape
    cols = 3 * hidden // CHUNKS
    bf16 = jnp.bfloat16
    return pl.pallas_call(
        sum_kernel,
        out_shape=jax.ShapeDtypeStruct((CHUNKS, rows, cols), bf16),
        in_specs=vmem(5),
        out_specs=vmem(1)[0],
        scratch_shapes=[
            pltpu.VMEM((cores, blocks * rows, shard), bf16),
            pltpu.VMEM((cores, blocks * rows, shard), bf16),
            pltpu.VMEM((CHUNKS, Z_WAYS, X_WAYS, rows, cols), bf16),
            pltpu.VMEM((CHUNKS, Z_WAYS, X_WAYS, rows, cols), bf16),
            pltpu.VMEM((CHUNKS, Z_WAYS, X_WAYS, rows, cols), bf16),
            pltpu.VMEM((CHUNKS, 2 * (X_WAYS - 1), rows, cols), bf16),
            pltpu.VMEM((CHUNKS, X_WAYS - 1, rows, cols), bf16),
            pltpu.SemaphoreType.DMA((CHUNKS, 7)),
            pltpu.SemaphoreType.DMA((CHUNKS, 7)),
        ],
        compiler_params=pltpu.CompilerParams(
            collective_id=0, has_side_effects=True, vmem_limit_bytes=50 << 20
        ),
    )(packed, w_gate, w_up, w_down, weight)


def spread_rows(inv_root, act, packed, w_gate, w_up):
    (blocks, cores, rows, width), (shard, hidden) = packed.shape, w_gate.shape
    cols = 3 * hidden // CHUNKS
    slots = cores * blocks * rows
    bf16 = jnp.bfloat16
    return pl.pallas_call(
        functools.partial(spread_kernel, inv_root),
        out_shape=(
            jax.ShapeDtypeStruct((shard, hidden), bf16),
            jax.ShapeDtypeStruct((shard, hidden), bf16),
            jax.ShapeDtypeStruct((shard, hidden), bf16),
            jax.ShapeDtypeStruct((blocks, cores, rows // 2, width), bf16),
        ),
        in_specs=vmem(4),
        out_specs=vmem(4),
        scratch_shapes=[
            pltpu.VMEM((shard, slots), bf16),
            pltpu.VMEM((shard, slots), bf16),
            pltpu.VMEM((CHUNKS, cores, Z_WAYS, X_WAYS, rows, cols), bf16),
            pltpu.VMEM((slots, shard), jnp.float32),
            pltpu.SemaphoreType.DMA((CHUNKS, 7)),
            pltpu.SemaphoreType.DMA((CHUNKS, 7)),
        ],
        compiler_params=pltpu.CompilerParams(
            collective_id=1, has_side_effects=True, vmem_limit_bytes=50 << 20
        ),
    )(act, packed, w_gate, w_up)


FAR_DP = ((2, 1), (1, 1), (3, 1), (2, 0), (0, 1), (1, 0), (3, 0))
FAR_EXPERT = ((2, 1), (1, 1), (3, 1), (2, 0), (1, 0), (3, 0), (0, 1))
Y_WAYS, PAIR = 4, 2


class Wide(Place):
    def __init__(self):
        super().__init__()
        self.d = (self.zh * X_WAYS + self.x) * CORES + self.c
        self.y, self.zl = self.expert % Y_WAYS, self.expert // Y_WAYS

    def dp(self, far, core):
        return ((self.zh + far[1]) % Z_WAYS * X_WAYS + (self.x + far[0]) % X_WAYS) * CORES + core

    def other(self, far):
        return (self.zl + far[1]) % PAIR * Y_WAYS + (self.y + far[0]) % Y_WAYS

    def greet(self):
        barrier = pltpu.get_barrier_semaphore()
        peers = [(self.other(far), self.d) for far in FAR_EXPERT]
        peers += [(self.expert, self.dp(far, core)) for far in FAR_DP for core in range(CORES)]
        peers.append(self.partner())
        for peer in peers:
            pl.semaphore_signal(barrier, inc=1, device_id=peer, device_id_type=MESH)
        pl.semaphore_wait(barrier, len(peers))


def remote(src, dst, send_sem, recv_sem, peer):
    return pltpu.make_async_remote_copy(
        src_ref=src, dst_ref=dst, send_sem=send_sem, recv_sem=recv_sem,
        device_id=peer, device_id_type=MESH,
    )


def dispatch_kernel(
    pick_ref, x_ref, g_ref, out_ref, tok, away, mid, send1, recv1, send2, recv2
):
    me = Wide()
    shard = x_ref.shape[1] // CORES
    for h in range(CORES):
        cols = slice(h * shard, (h + 1) * shard)
        tok[h] = jnp.concatenate([x_ref[:, cols], g_ref[:, cols]], axis=1)
    me.greet()

    def picked(e, h):
        return jnp.dot(pick_ref[e], tok[h], preferred_element_type=jnp.float32).astype(jnp.bfloat16)

    def to_expert(h, k):
        e = me.other(FAR_EXPERT[k])
        return remote(
            away.at[h, e], mid.at[h, me.expert], send1.at[h, k], recv1.at[h, me.expert], (e, me.d)
        )

    def to_shard(h, k, d):
        return remote(
            mid.at[h, d // CORES], out_ref.at[me.d // CORES, me.c], send2.at[h, k], recv2.at[me.d],
            (me.expert, d),
        )

    for h in range(CORES):
        for k, far in enumerate(FAR_EXPERT):
            e = me.other(far)
            away[h, e] = picked(e, h)
            to_expert(h, k).start()
        mid[h, me.expert] = picked(me.expert, h)

    for h in range(CORES):
        for k, far in enumerate(FAR_DP + ((0, 0),)):
            d = me.dp(far, h)
            src = d // CORES

            @pl.when(src != me.expert)
            def _():
                remote(
                    away.at[h, src], mid.at[h, src], send1.at[h, 0], recv1.at[h, src], (src, me.d)
                ).wait_recv()

            if far != (0, 0):
                to_shard(h, k, d).start()
            else:

                @pl.when(me.c != h)
                def _():
                    to_shard(h, k, d).start()

                @pl.when(me.c == h)
                def _():
                    out_ref[me.d // CORES, me.c] = mid[h, src]

    def from_source(d):
        return remote(mid.at[0, 0], out_ref.at[d // CORES, d % CORES], send2.at[0, 0], recv2.at[d], (me.expert, d))

    for far in FAR_DP:
        for core in range(CORES):
            from_source(me.dp(far, core)).wait_recv()
    from_source(me.dp((0, 0), 1 - me.c)).wait_recv()
    for h in range(CORES):
        for k, far in enumerate(FAR_EXPERT):
            to_expert(h, k).wait_send()
        for k, far in enumerate(FAR_DP):
            to_shard(h, k, me.dp(far, h)).wait_send()

        @pl.when(me.c != h)
        def _():
            to_shard(h, len(FAR_DP), me.dp((0, 0), h)).wait_send()


def return_kernel(
    low_ref, high_ref, dx_ref, out_ref, mid, back, send1, recv1, send2, recv2
):
    me = Wide()
    me.greet()
    shard = out_ref.shape[1] // CORES
    near = me.dp((0, 0), 1 - me.c)

    def to_block(k, d):
        return remote(
            dx_ref.at[d // CORES, d % CORES], mid.at[me.d // CORES, me.c], send1.at[k], recv1.at[me.d],
            (me.expert, d),
        )

    def to_features(k):
        e = me.other(FAR_EXPERT[k])
        return remote(mid.at[e], back.at[me.expert], send2.at[k], recv2.at[me.expert], (e, me.d))

    targets = [me.dp(far, core) for far in FAR_DP for core in range(CORES)] + [near]
    for k, d in enumerate(targets):
        to_block(k, d).start()
    mid[me.d // CORES, me.c] = dx_ref[me.d // CORES, me.c]

    def arrived(e):
        for core in range(CORES):
            d = e * CORES + core

            @pl.when(d != me.d)
            def _():
                remote(
                    dx_ref.at[0, 0], mid.at[e, core], send1.at[0], recv1.at[d], (me.expert, d)
                ).wait_recv()

    for k, far in enumerate(FAR_EXPERT):
        arrived(me.other(far))
        to_features(k).start()
    arrived(me.expert)
    back[me.expert] = mid[me.expert]
    for far in FAR_EXPERT:
        e = me.other(far)
        remote(mid.at[0], back.at[e], send2.at[0], recv2.at[e], (e, me.d)).wait_recv()
    parts = []
    for h in range(CORES):
        rows = back[:, h].reshape(low_ref.shape[1], CORES * shard)
        low = jnp.dot(low_ref[...], rows, preferred_element_type=jnp.float32)
        high = jnp.dot(high_ref[...], rows, preferred_element_type=jnp.float32)
        parts.append(low[:, :shard] + high[:, shard:])
    out_ref[...] = jnp.concatenate(parts, axis=1).astype(jnp.bfloat16)
    for k, d in enumerate(targets):
        to_block(k, d).wait_send()
    for k in range(len(FAR_EXPERT)):
        to_features(k).wait_send()


def dispatched(pick, x, g):
    (experts, rows, _), (tokens, width) = pick.shape, x.shape
    bf16 = jnp.bfloat16
    groups = X_WAYS * Z_WAYS
    dma = pltpu.SemaphoreType.DMA
    return pl.pallas_call(
        dispatch_kernel,
        out_shape=jax.ShapeDtypeStruct((groups, CORES, rows, width), bf16),
        in_specs=vmem(3),
        out_specs=vmem(1)[0],
        scratch_shapes=[
            pltpu.VMEM((CORES, tokens, width), bf16),
            pltpu.VMEM((CORES, experts, rows, width), bf16),
            pltpu.VMEM((CORES, experts, rows, width), bf16),
            dma((CORES, len(FAR_EXPERT))),
            dma((CORES, experts)),
            dma((CORES, len(FAR_DP) + 1)),
            dma((groups * CORES,)),
        ],
        compiler_params=pltpu.CompilerParams(
            collective_id=2, has_side_effects=True, vmem_limit_bytes=20 << 20
        ),
    )(pick, x, g)


def returned_rows(low, high, dx):
    groups, cores, rows, width = dx.shape
    tokens, bf16 = low.shape[0], jnp.bfloat16
    experts = Y_WAYS * PAIR
    dma = pltpu.SemaphoreType.DMA
    return pl.pallas_call(
        return_kernel,
        out_shape=jax.ShapeDtypeStruct((tokens, width), bf16),
        in_specs=vmem(3),
        out_specs=vmem(1)[0],
        scratch_shapes=[
            pltpu.VMEM((experts, cores, rows, width), bf16),
            pltpu.VMEM((experts, cores, rows, width), bf16),
            dma((groups * cores,)),
            dma((groups * cores,)),
            dma((len(FAR_EXPERT),)),
            dma((experts,)),
        ],
        compiler_params=pltpu.CompilerParams(
            collective_id=3, has_side_effects=True, vmem_limit_bytes=20 << 20
        ),
    )(low, high, dx)


def body(tokens, grad_out, expert_ids, route_weights, w_gate, w_up, w_down):
    experts = lax.axis_size("expert")
    groups = lax.axis_size("dp")
    tok_rows = tokens.shape[0]
    capacity = tok_rows // 2
    expert_index = lax.axis_index("expert")
    inv_root = 1.0 / math.sqrt(tok_rows * groups)
    gate_shard, up_shard, down_shard = w_gate[0], w_up[0], w_down[0].T

    names = jnp.arange(experts, dtype=jnp.int32)[:, None]
    hit0 = expert_ids[:, 0][None, :] == names
    hit1 = expert_ids[:, 1][None, :] == names
    hit = (hit0 | hit1).astype(jnp.bfloat16)
    index = jnp.arange(tok_rows, dtype=jnp.int32)
    before = (index[:, None] < index[None, :]).astype(jnp.bfloat16)
    rank = jnp.dot(hit, before, preferred_element_type=jnp.float32)
    rank = jnp.where(hit > 0, rank, -1.0).astype(jnp.int32)
    chosen = rank[:, None, :] == jnp.arange(capacity, dtype=jnp.int32)[None, :, None]
    pick = chosen.astype(jnp.bfloat16)

    def place(first):
        part = rank.T[:, :, None] == jnp.arange(first, first + capacity // 2, dtype=jnp.int32)
        return part.astype(jnp.bfloat16).reshape(tok_rows, experts * capacity // 2)

    weight_of = jnp.where(hit0, route_weights[:, 0][None, :], 0.0) + jnp.where(
        hit1, route_weights[:, 1][None, :], 0.0
    )
    own_rank = lax.dynamic_slice_in_dim(rank, expert_index, 1)
    own_weight_of = lax.dynamic_slice_in_dim(weight_of, expert_index, 1)
    own_weight = jnp.sum(
        jnp.where(
            own_rank == jnp.arange(capacity, dtype=jnp.int32)[:, None], own_weight_of, 0.0
        ),
        axis=1,
    )

    packed = dispatched(pick, tokens, grad_out)
    act = summed_rows(packed, gate_shard, up_shard, down_shard, own_weight[:, None])
    grad_g, grad_u, grad_d, dx_rows = spread_rows(inv_root, act, packed, gate_shard, up_shard)
    grad_tokens = returned_rows(place(0), place(capacity // 2), dx_rows)
    return (grad_tokens, grad_g[None], grad_u[None], grad_d.T[None])


def solution(mesh):
    in_specs = (
        P("dp", "expert"),
        P("dp", "expert"),
        P("dp", None),
        P("dp", None),
        P("expert", "dp", None),
        P("expert", "dp", None),
        P("expert", None, "dp"),
    )
    out_specs = (
        P("dp", "expert"),
        P("expert", "dp", None),
        P("expert", "dp", None),
        P("expert", None, "dp"),
    )
    return jax.shard_map(body, mesh=mesh, in_specs=in_specs, out_specs=out_specs, check_vma=False)
```

```python
import functools
import math

import jax
import jax.numpy as jnp
from jax import lax
from jax.experimental import pallas as pl
from jax.experimental.pallas import tpu as pltpu
from jax.sharding import PartitionSpec as P

MESH = pl.DeviceIdType.MESH
CHUNKS = 8
X_WAYS, Z_WAYS, CORES = 4, 2, 2
LAST = (((1,), (1,)), ((), ()))
SUM_ORDER = "zxzxzxzx"
SPREAD_ORDER = "xzxzxzxzxzxz"
SUM_LAGS = (0, 1, 3, 4, 6)
SPREAD_LAGS = (0, 1, 3, 4)


class Place:
    def __init__(self):
        self.expert = lax.axis_index("expert")
        d = lax.axis_index("dp")
        self.c = d % CORES
        self.x = (d // CORES) % X_WAYS
        self.zh = d // (CORES * X_WAYS)

    def at(self, zh, x, c):
        return (self.expert, (zh * X_WAYS + x) * CORES + c)

    def partner(self):
        return self.at(self.zh, self.x, 1 - self.c)

    def opposite(self):
        return self.at(1 - self.zh, self.x, self.c)

    def along_x(self, k):
        return (self.x + k) % X_WAYS

    def ring(self, k):
        return self.at(self.zh, self.along_x(k), self.c)

    def greet(self):
        barrier = pltpu.get_barrier_semaphore()
        peers = [self.partner(), self.opposite()] + [self.ring(k) for k in range(1, X_WAYS)]
        for peer in peers:
            pl.semaphore_signal(barrier, inc=1, device_id=peer, device_id_type=MESH)
        pl.semaphore_wait(barrier, len(peers))


def remote(src, dst, send_sem, recv_sem, peer):
    return pltpu.make_async_remote_copy(
        src_ref=src, dst_ref=dst, send_sem=send_sem, recv_sem=recv_sem,
        device_id=peer, device_id_type=MESH,
    )


def sum_kernel(
    rows_ref, wg_ref, wu_ref, wd_ref, pw_ref, out_ref,
    xp, gp, away, arrived, held, first, second, send_sem, recv_sem,
):
    me = Place()
    me.greet()
    n = wg_ref.shape[1] // CHUNKS
    blocks, rows, shard = X_WAYS * Z_WAYS, rows_ref.shape[2], wg_ref.shape[0]
    low, high = pl.ds(0, rows // 2), pl.ds(rows // 2, rows // 2)
    here, up, down, far = me.x, me.along_x(1), me.along_x(3), me.along_x(2)
    f32 = jnp.float32

    for i in range(blocks):
        at = pl.ds(i * rows, rows)
        for which in range(CORES):
            both = rows_ref[i, me.c if which == 0 else 1 - me.c]
            xp[which, at, :] = both[:, :shard]
            gp[which, at, :] = both[:, shard:]

    def copy(j, lane, src, dst, peer):
        return remote(src, dst, send_sem.at[j, lane], recv_sem.at[j, lane], peer)

    def add(ref, more):
        ref[...] = (ref[...].astype(f32) + more.astype(f32)).astype(jnp.bfloat16)

    def products(j, which, dst):
        cols = pl.ds(j * n, n)
        parts = (
            jnp.dot(xp[which], wg_ref[:, cols], preferred_element_type=f32),
            jnp.dot(xp[which], wu_ref[:, cols], preferred_element_type=f32),
            jnp.dot(gp[which], wd_ref[:, cols], preferred_element_type=f32),
        )
        for k, part in enumerate(parts):
            dst[j, :, :, :, k * n : (k + 1) * n] = part.astype(jnp.bfloat16).reshape(
                Z_WAYS, X_WAYS, rows, n
            )

    def to_partner(j):
        return copy(j, 0, away.at[j], arrived.at[j], me.partner())

    def opposite(j):
        if SUM_ORDER[j] == "x":
            return copy(j, 1, held.at[j, 1 - me.zh, here], first.at[j, 4], me.opposite())
        return copy(j, 1, held.at[j, 1 - me.zh], first.at[j, pl.ds(0, X_WAYS)], me.opposite())

    def ring_first(j, lanes=(0, 1, 2, 3)):
        mine = held.at[j, me.zh]
        if SUM_ORDER[j] == "x":
            table = (
                (held.at[j, 0, far], first.at[j, 0]),
                (held.at[j, 1, far], first.at[j, 1]),
                (held.at[j, 1, up], first.at[j, 2]),
                (held.at[j, 0, down], first.at[j, 3]),
            )
        else:
            table = (
                (mine.at[far, low], second.at[j, 2, low]),
                (mine.at[far, high], second.at[j, 2, high]),
                (mine.at[up, high], second.at[j, 0, high]),
                (mine.at[down, low], second.at[j, 1, low]),
            )
        return [copy(j, 2 + i, *table[i], me.ring(1 + 2 * (i % 2))) for i in lanes]

    def ring_second(j):
        if SUM_ORDER[j] == "x":
            return [
                copy(j, 6, held.at[j, 0, up], second.at[j, 0], me.ring(1)),
                copy(j, 7, held.at[j, 1, down], second.at[j, 1], me.ring(3)),
            ]
        mine = held.at[j, me.zh]
        return [
            copy(j, 6, mine.at[up, low], second.at[j, 0, low], me.ring(1)),
            copy(j, 7, mine.at[down, high], second.at[j, 1, high], me.ring(3)),
        ]

    def arrive(copies):
        for one in copies:
            one.wait_recv()

    def start(copies):
        for one in copies:
            one.start()

    def make(j):
        products(j, 1, away)
        to_partner(j).start()
        products(j, 0, held)

    def cores(j):
        arrive([to_partner(j)])
        for z in range(Z_WAYS):
            add(held.at[j, z], arrived[j, z])
        start(ring_first(j) if SUM_ORDER[j] == "x" else [opposite(j)])

    def pass_on(j):
        copies = ring_second(j)
        if SUM_ORDER[j] == "x":
            arrive(ring_first(j, (0,)))
            add(held.at[j, 0, up], first[j, 0])
            copies[0].start()
            arrive(ring_first(j, (1,)))
            add(held.at[j, 1, down], first[j, 1])
            copies[1].start()
        else:
            arrive(ring_first(j, (0,)))
            add(held.at[j, me.zh, up, low], second[j, 2, low])
            copies[0].start()
            arrive(ring_first(j, (1,)))
            add(held.at[j, me.zh, down, high], second[j, 2, high])
            copies[1].start()

    def gather(j):
        if SUM_ORDER[j] == "x":
            arrive(ring_first(j, (2, 3)) + ring_second(j))
            for z, (one, two) in enumerate(((second.at[j, 0], first.at[j, 3]), (second.at[j, 1], first.at[j, 2]))):
                add(held.at[j, z, here], one[...].astype(f32) + two[...].astype(f32))
            start([opposite(j)])
        else:
            arrive([opposite(j)])
            for x in (me.along_x(2), me.along_x(1), me.along_x(3), me.x):
                add(held.at[j, me.zh, x], first[j, x])
            start(ring_first(j))

    def finish(j):
        total = held[j, me.zh, here].astype(f32)
        if SUM_ORDER[j] == "x":
            arrive([opposite(j)])
            total += first[j, 4].astype(f32)
        else:
            arrive(ring_first(j, (2, 3)) + ring_second(j))
            total += second[j, 0].astype(f32) + second[j, 1].astype(f32)
        weight = pw_ref[...]
        gate, upper, back = total[:, :n], total[:, n : 2 * n], total[:, 2 * n :] * weight
        s = 1.0 / (1.0 + jnp.exp(-gate))
        out_ref[j, :, :n] = (back * upper * s * (1.0 + gate * (1.0 - s))).astype(jnp.bfloat16)
        out_ref[j, :, n:] = (back * gate * s).astype(jnp.bfloat16)
        at = (j % 2) * n
        out_ref[CHUNKS + j // 2, :, at : at + n] = (weight * gate * s * upper).astype(jnp.bfloat16)

    def middle(j, step):
        order = (pass_on, gather) if SUM_ORDER[j] == "x" else (gather, pass_on)
        order[step](j)

    stages = (make, cores, lambda j: middle(j, 0), lambda j: middle(j, 1), finish)
    for t in range(CHUNKS + SUM_LAGS[-1]):
        for stage, lag in zip(stages, SUM_LAGS):
            if 0 <= t - lag < CHUNKS:
                stage(t - lag)
    for j in range(CHUNKS):
        for one in [to_partner(j), opposite(j)] + ring_first(j) + ring_second(j):
            one.wait_send()


def vmem(count):
    return [pl.BlockSpec(memory_space=pltpu.VMEM)] * count


def summed_rows(packed, w_gate, w_up, w_down, weight):
    (blocks, cores, rows, _), (shard, hidden) = packed.shape, w_gate.shape
    cols = 3 * hidden // CHUNKS
    bf16 = jnp.bfloat16
    return pl.pallas_call(
        sum_kernel,
        out_shape=jax.ShapeDtypeStruct((CHUNKS * 3 // 2, rows, 2 * hidden // CHUNKS), bf16),
        in_specs=vmem(5),
        out_specs=vmem(1)[0],
        scratch_shapes=[
            pltpu.VMEM((cores, blocks * rows, shard), bf16),
            pltpu.VMEM((cores, blocks * rows, shard), bf16),
            pltpu.VMEM((CHUNKS, Z_WAYS, X_WAYS, rows, cols), bf16),
            pltpu.VMEM((CHUNKS, Z_WAYS, X_WAYS, rows, cols), bf16),
            pltpu.VMEM((CHUNKS, Z_WAYS, X_WAYS, rows, cols), bf16),
            pltpu.VMEM((CHUNKS, X_WAYS + 1, rows, cols), bf16),
            pltpu.VMEM((CHUNKS, X_WAYS - 1, rows, cols), bf16),
            pltpu.SemaphoreType.DMA((CHUNKS, 8)),
            pltpu.SemaphoreType.DMA((CHUNKS, 8)),
        ],
        compiler_params=pltpu.CompilerParams(
            collective_id=0, has_side_effects=True, vmem_limit_bytes=50 << 20
        ),
    )(packed, w_gate, w_up, w_down, weight)


FAR_DP = ((2, 1), (1, 1), (3, 1), (2, 0), (0, 1), (1, 0), (3, 0))
FAR_EXPERT = ((2, 1), (1, 1), (3, 1), (2, 0), (1, 0), (3, 0), (0, 1))
Y_WAYS, PAIR = 4, 2


class Wide(Place):
    def __init__(self):
        super().__init__()
        self.d = (self.zh * X_WAYS + self.x) * CORES + self.c
        self.y, self.zl = self.expert % Y_WAYS, self.expert // Y_WAYS

    def dp(self, far, core):
        return ((self.zh + far[1]) % Z_WAYS * X_WAYS + (self.x + far[0]) % X_WAYS) * CORES + core

    def other(self, far):
        return (self.zl + far[1]) % PAIR * Y_WAYS + (self.y + far[0]) % Y_WAYS

    def greet(self):
        barrier = pltpu.get_barrier_semaphore()
        peers = [(self.other(far), self.d) for far in FAR_EXPERT]
        peers += [(self.expert, self.dp(far, core)) for far in FAR_DP for core in range(CORES)]
        peers.append(self.partner())
        for peer in peers:
            pl.semaphore_signal(barrier, inc=1, device_id=peer, device_id_type=MESH)
        pl.semaphore_wait(barrier, len(peers))


def dispatch_kernel(
    pick_ref, x_ref, g_ref, out_ref, tok, away, mid, send1, recv1, send2, recv2
):
    me = Wide()
    shard = x_ref.shape[1] // CORES
    for h in range(CORES):
        cols = slice(h * shard, (h + 1) * shard)
        tok[h] = jnp.concatenate([x_ref[:, cols], g_ref[:, cols]], axis=1)
    me.greet()

    def picked(e, h):
        return jnp.dot(pick_ref[e], tok[h], preferred_element_type=jnp.float32).astype(jnp.bfloat16)

    def to_expert(h, k):
        e = me.other(FAR_EXPERT[k])
        return remote(
            away.at[h, e], mid.at[h, me.expert], send1.at[h, k], recv1.at[h, me.expert], (e, me.d)
        )

    def to_shard(h, k, d):
        return remote(
            mid.at[h, d // CORES], out_ref.at[me.d // CORES, me.c], send2.at[h, k], recv2.at[me.d],
            (me.expert, d),
        )

    for h in range(CORES):
        for k, far in enumerate(FAR_EXPERT):
            e = me.other(far)
            away[h, e] = picked(e, h)
            to_expert(h, k).start()
        mid[h, me.expert] = picked(me.expert, h)

    for h in range(CORES):
        for k, far in enumerate(FAR_DP + ((0, 0),)):
            d = me.dp(far, h)
            src = d // CORES

            @pl.when(src != me.expert)
            def _():
                remote(
                    away.at[h, src], mid.at[h, src], send1.at[h, 0], recv1.at[h, src], (src, me.d)
                ).wait_recv()

            if far != (0, 0):
                to_shard(h, k, d).start()
            else:

                @pl.when(me.c != h)
                def _():
                    to_shard(h, k, d).start()

                @pl.when(me.c == h)
                def _():
                    out_ref[me.d // CORES, me.c] = mid[h, src]

    def from_source(d):
        return remote(mid.at[0, 0], out_ref.at[d // CORES, d % CORES], send2.at[0, 0], recv2.at[d], (me.expert, d))

    for far in FAR_DP:
        for core in range(CORES):
            from_source(me.dp(far, core)).wait_recv()
    from_source(me.dp((0, 0), 1 - me.c)).wait_recv()
    for h in range(CORES):
        for k, far in enumerate(FAR_EXPERT):
            to_expert(h, k).wait_send()
        for k, far in enumerate(FAR_DP):
            to_shard(h, k, me.dp(far, h)).wait_send()

        @pl.when(me.c != h)
        def _():
            to_shard(h, len(FAR_DP), me.dp((0, 0), h)).wait_send()


def spread_kernel(
    inv_root, act_ref, rows_ref, wg_ref, wu_ref, low_ref, high_ref, gg_ref, gu_ref, gd_ref, out_ref,
    xt, gt, whole, total, dx, mid, back, send_sem, recv_sem, send1, recv1, send2, recv2,
):
    me = Wide()
    me.greet()
    n = wg_ref.shape[1] // CHUNKS
    blocks, rows, shard = X_WAYS * Z_WAYS, rows_ref.shape[2], wg_ref.shape[0]
    slots = CORES * blocks * rows
    low, high = pl.ds(0, rows // 2), pl.ds(rows // 2, rows // 2)
    here, up, down = me.x, me.along_x(1), me.along_x(3)
    f32 = jnp.float32
    spread_chunks = len(SPREAD_ORDER)

    def copy(j, lane, src, dst, peer):
        return remote(src, dst, send_sem.at[j, lane], recv_sem.at[j, lane], peer)

    def part(j, x, half=None):
        if half is None:
            return whole.at[j, 0, me.zh, x] if SPREAD_ORDER[j] == "x" else whole.at[j, 0, :, x]
        return whole.at[j, 0, me.zh, x, half] if SPREAD_ORDER[j] == "x" else whole.at[j, 0, :, x, half]

    def neighbours(j):
        src = act_ref.at[j] if SPREAD_ORDER[j] == "x" else part(j, here)
        return [copy(j, 2, src, part(j, here), me.ring(1)), copy(j, 3, src, part(j, here), me.ring(3))]

    def passed(j):
        return [
            copy(j, 4, part(j, down, low), part(j, down, low), me.ring(1)),
            copy(j, 5, part(j, up, high), part(j, up, high), me.ring(3)),
        ]

    def opposite(j):
        if SPREAD_ORDER[j] == "x":
            return copy(j, 1, whole.at[j, 0, me.zh], whole.at[j, 0, me.zh], me.opposite())
        return copy(j, 1, act_ref.at[j], whole.at[j, 0, me.zh, here], me.opposite())

    def to_partner(j):
        return copy(j, 0, whole.at[j, 0], whole.at[j, 1], me.partner())

    def begin(j):
        if SPREAD_ORDER[j] == "x":
            for one in neighbours(j):
                one.start()
        else:
            opposite(j).start()
        whole[j, 0, me.zh, here] = act_ref[j]

    def relay(j):
        for one, on in zip(neighbours(j), passed(j)):
            one.wait_recv()
            on.start()

    def middle(j, step):
        if SPREAD_ORDER[j] == "x":
            if step == 0:
                relay(j)
            else:
                for one in passed(j):
                    one.wait_recv()
                opposite(j).start()
        elif step == 0:
            opposite(j).wait_recv()
            for one in neighbours(j):
                one.start()
        else:
            relay(j)

    def cores(j):
        if SPREAD_ORDER[j] == "x":
            opposite(j).wait_recv()
        else:
            for one in passed(j):
                one.wait_recv()
        to_partner(j).start()

    def grad(turned, j, cols):
        both = whole[j, :, :, :, :, cols].reshape(slots, -1)
        return (jnp.dot(turned[...], both, preferred_element_type=f32) * inv_root).astype(jnp.bfloat16)

    def inputs(j):
        to_partner(j).wait_recv()
        cols = pl.ds(j * n, n)
        d_gate = whole[j, :, :, :, :, :n].reshape(slots, n)
        d_up = whole[j, :, :, :, :, n:].reshape(slots, n)
        more = lax.dot_general(d_gate, wg_ref[:, cols], LAST, preferred_element_type=f32)
        more += lax.dot_general(d_up, wu_ref[:, cols], LAST, preferred_element_type=f32)
        total[...] = more if j == 0 else total[...] + more

    def weights(j):
        if j < CHUNKS:
            cols = pl.ds(j * n, n)
            gg_ref[:, cols] = grad(xt, j, slice(0, n))
            gu_ref[:, cols] = grad(xt, j, slice(n, 2 * n))
        else:
            to_partner(j).wait_recv()
            gd_ref[:, pl.ds((j - CHUNKS) * 2 * n, 2 * n)] = grad(gt, j, slice(0, 2 * n))

    near = me.dp((0, 0), 1 - me.c)
    targets = [me.dp(far, core) for far in FAR_DP for core in range(CORES)] + [near]

    def to_block(k, d):
        return remote(
            dx.at[d // CORES, d % CORES], mid.at[me.d // CORES, me.c], send1.at[k], recv1.at[me.d],
            (me.expert, d),
        )

    def to_features(k):
        e = me.other(FAR_EXPERT[k])
        return remote(mid.at[e], back.at[me.expert], send2.at[k], recv2.at[me.expert], (e, me.d))

    def home_first():
        for i in range(blocks):
            for which in range(CORES):
                at = (which * blocks + i) * rows
                one = total[at : at + rows // 2, :].astype(jnp.bfloat16)
                two = total[at + rows // 2 : at + rows, :].astype(jnp.bfloat16)
                dx[i, me.c if which == 0 else 1 - me.c] = jnp.concatenate([one, two], axis=1)
        for k, d in enumerate(targets):
            to_block(k, d).start()
        mid[me.d // CORES, me.c] = dx[me.d // CORES, me.c]

    def arrived(e):
        for core in range(CORES):
            d = e * CORES + core

            @pl.when(d != me.d)
            def _():
                remote(
                    dx.at[0, 0], mid.at[e, core], send1.at[0], recv1.at[d], (me.expert, d)
                ).wait_recv()

    def home_second():
        for k, far in enumerate(FAR_EXPERT):
            arrived(me.other(far))
            to_features(k).start()
        arrived(me.expert)
        back[me.expert] = mid[me.expert]

    def home():
        for far in FAR_EXPERT:
            e = me.other(far)
            remote(mid.at[0], back.at[e], send2.at[0], recv2.at[e], (e, me.d)).wait_recv()
        parts = []
        for h in range(CORES):
            blocks_of = back[:, h].reshape(low_ref.shape[1], CORES * shard)
            one = jnp.dot(low_ref[...], blocks_of, preferred_element_type=f32)
            two = jnp.dot(high_ref[...], blocks_of, preferred_element_type=f32)
            parts.append(one[:, :shard] + two[:, shard:])
        out_ref[...] = jnp.concatenate(parts, axis=1).astype(jnp.bfloat16)

    for j in range(spread_chunks):
        begin(j)
    for lo, turned in ((0, xt), (shard, gt)):
        for i in range(blocks):
            for which in range(CORES):
                at = pl.ds((which * blocks + i) * rows, rows)
                c = me.c if which == 0 else 1 - me.c
                total[at, :] = rows_ref[i, c][:, lo : lo + shard].astype(f32)
        turned[...] = total[...].T.astype(jnp.bfloat16)

    def products(j):
        if j < CHUNKS:
            inputs(j)
        if j == CHUNKS - 1:
            home_first()
        if j < CHUNKS:
            weights(j)

    stages = (lambda j: middle(j, 0), lambda j: middle(j, 1), cores, products)
    for t in range(spread_chunks + SPREAD_LAGS[-1]):
        for stage, lag in zip(stages, SPREAD_LAGS):
            if 0 <= t - lag < spread_chunks:
                stage(t - lag)
    home_second()
    for j in range(CHUNKS, spread_chunks):
        weights(j)
    home()
    for j in range(spread_chunks):
        for one in [to_partner(j), opposite(j)] + neighbours(j) + passed(j):
            one.wait_send()
    for k, d in enumerate(targets):
        to_block(k, d).wait_send()
    for k in range(len(FAR_EXPERT)):
        to_features(k).wait_send()


def dispatched(pick, x, g):
    (experts, rows, _), (tokens, width) = pick.shape, x.shape
    bf16 = jnp.bfloat16
    groups = X_WAYS * Z_WAYS
    dma = pltpu.SemaphoreType.DMA
    return pl.pallas_call(
        dispatch_kernel,
        out_shape=jax.ShapeDtypeStruct((groups, CORES, rows, width), bf16),
        in_specs=vmem(3),
        out_specs=vmem(1)[0],
        scratch_shapes=[
            pltpu.VMEM((CORES, tokens, width), bf16),
            pltpu.VMEM((CORES, experts, rows, width), bf16),
            pltpu.VMEM((CORES, experts, rows, width), bf16),
            dma((CORES, len(FAR_EXPERT))),
            dma((CORES, experts)),
            dma((CORES, len(FAR_DP) + 1)),
            dma((groups * CORES,)),
        ],
        compiler_params=pltpu.CompilerParams(
            collective_id=2, has_side_effects=True, vmem_limit_bytes=20 << 20
        ),
    )(pick, x, g)


def spread_rows(inv_root, act, packed, w_gate, w_up, low, high):
    (blocks, cores, rows, width), (shard, hidden) = packed.shape, w_gate.shape
    cols = 2 * hidden // CHUNKS
    slots = cores * blocks * rows
    experts = Y_WAYS * PAIR
    count = len(SPREAD_ORDER)
    bf16, dma = jnp.bfloat16, pltpu.SemaphoreType.DMA
    return pl.pallas_call(
        functools.partial(spread_kernel, inv_root),
        out_shape=(
            jax.ShapeDtypeStruct((shard, hidden), bf16),
            jax.ShapeDtypeStruct((shard, hidden), bf16),
            jax.ShapeDtypeStruct((shard, hidden), bf16),
            jax.ShapeDtypeStruct((low.shape[0], width), bf16),
        ),
        in_specs=vmem(6),
        out_specs=vmem(4),
        scratch_shapes=[
            pltpu.VMEM((shard, slots), bf16),
            pltpu.VMEM((shard, slots), bf16),
            pltpu.VMEM((count, cores, Z_WAYS, X_WAYS, rows, cols), bf16),
            pltpu.VMEM((slots, shard), jnp.float32),
            pltpu.VMEM((blocks, cores, rows // 2, width), bf16),
            pltpu.VMEM((experts, cores, rows // 2, width), bf16),
            pltpu.VMEM((experts, cores, rows // 2, width), bf16),
            dma((count, 6)),
            dma((count, 6)),
            dma((blocks * cores,)),
            dma((blocks * cores,)),
            dma((len(FAR_EXPERT),)),
            dma((experts,)),
        ],
        compiler_params=pltpu.CompilerParams(
            collective_id=1, has_side_effects=True, vmem_limit_bytes=50 << 20
        ),
    )(act, packed, w_gate, w_up, low, high)


def body(tokens, grad_out, expert_ids, route_weights, w_gate, w_up, w_down):
    experts = lax.axis_size("expert")
    groups = lax.axis_size("dp")
    tok_rows = tokens.shape[0]
    capacity = tok_rows // 2
    expert_index = lax.axis_index("expert")
    inv_root = 1.0 / math.sqrt(tok_rows * groups)
    gate_shard, up_shard, down_shard = w_gate[0], w_up[0], w_down[0].T

    names = jnp.arange(experts, dtype=jnp.int32)[:, None]
    hit0 = expert_ids[:, 0][None, :] == names
    hit1 = expert_ids[:, 1][None, :] == names
    hit = (hit0 | hit1).astype(jnp.bfloat16)
    index = jnp.arange(tok_rows, dtype=jnp.int32)
    before = (index[:, None] < index[None, :]).astype(jnp.bfloat16)
    rank = jnp.dot(hit, before, preferred_element_type=jnp.float32)
    rank = jnp.where(hit > 0, rank, -1.0).astype(jnp.int32)
    chosen = rank[:, None, :] == jnp.arange(capacity, dtype=jnp.int32)[None, :, None]
    pick = chosen.astype(jnp.bfloat16)

    def place(first):
        part = rank.T[:, :, None] == jnp.arange(first, first + capacity // 2, dtype=jnp.int32)
        return part.astype(jnp.bfloat16).reshape(tok_rows, experts * capacity // 2)

    weight_of = jnp.where(hit0, route_weights[:, 0][None, :], 0.0) + jnp.where(
        hit1, route_weights[:, 1][None, :], 0.0
    )
    own_rank = lax.dynamic_slice_in_dim(rank, expert_index, 1)
    own_weight_of = lax.dynamic_slice_in_dim(weight_of, expert_index, 1)
    own_weight = jnp.sum(
        jnp.where(
            own_rank == jnp.arange(capacity, dtype=jnp.int32)[:, None], own_weight_of, 0.0
        ),
        axis=1,
    )

    packed = dispatched(pick, tokens, grad_out)
    act = summed_rows(packed, gate_shard, up_shard, down_shard, own_weight[:, None])
    grad_g, grad_u, grad_d, grad_tokens = spread_rows(
        inv_root, act, packed, gate_shard, up_shard, place(0), place(capacity // 2)
    )
    return (grad_tokens, grad_g[None], grad_u[None], grad_d.T[None])


def solution(mesh):
    in_specs = (
        P("dp", "expert"),
        P("dp", "expert"),
        P("dp", None),
        P("dp", None),
        P("expert", "dp", None),
        P("expert", "dp", None),
        P("expert", None, "dp"),
    )
    out_specs = (
        P("dp", "expert"),
        P("expert", "dp", None),
        P("expert", "dp", None),
        P("expert", None, "dp"),
    )
    return jax.shard_map(body, mesh=mesh, in_specs=in_specs, out_specs=out_specs, check_vma=False)
```

```python
import functools
import math

import jax
import jax.numpy as jnp
from jax import lax
from jax.experimental import pallas as pl
from jax.experimental.pallas import tpu as pltpu
from jax.sharding import PartitionSpec as P

MESH = pl.DeviceIdType.MESH
CHUNKS = 8
X_WAYS, Z_WAYS, CORES = 4, 2, 2
LAST = (((1,), (1,)), ((), ()))
SUM_ORDER = "xzxzxzxx"
SPREAD_ORDER = "zxzxzzxzxzxz"
SUM_LAGS = (0, 1, 5, 7, 9)
SPREAD_LAGS = (0, 2, 4, 5)
LATE_LAG = 8


class Place:
    def __init__(self):
        self.expert = lax.axis_index("expert")
        d = lax.axis_index("dp")
        self.c = d % CORES
        self.x = (d // CORES) % X_WAYS
        self.zh = d // (CORES * X_WAYS)

    def at(self, zh, x, c):
        return (self.expert, (zh * X_WAYS + x) * CORES + c)

    def partner(self):
        return self.at(self.zh, self.x, 1 - self.c)

    def opposite(self):
        return self.at(1 - self.zh, self.x, self.c)

    def along_x(self, k):
        return (self.x + k) % X_WAYS

    def ring(self, k):
        return self.at(self.zh, self.along_x(k), self.c)

    def greet(self):
        barrier = pltpu.get_barrier_semaphore()
        peers = [self.partner(), self.opposite(), self.ring(1), self.ring(3)]
        for peer in peers:
            pl.semaphore_signal(barrier, inc=1, device_id=peer, device_id_type=MESH)
        pl.semaphore_wait(barrier, len(peers))


def remote(src, dst, send_sem, recv_sem, peer):
    return pltpu.make_async_remote_copy(
        src_ref=src, dst_ref=dst, send_sem=send_sem, recv_sem=recv_sem,
        device_id=peer, device_id_type=MESH,
    )


def sum_kernel(
    rows_ref, wg_ref, wu_ref, wd_ref, pw_ref, out_ref,
    xp, gp, away, arrived, held, first, second, send_sem, recv_sem,
):
    me = Place()
    me.greet()
    n = wg_ref.shape[1] // CHUNKS
    blocks, rows, shard = X_WAYS * Z_WAYS, rows_ref.shape[2], wg_ref.shape[0]
    low, high = pl.ds(0, rows // 2), pl.ds(rows // 2, rows // 2)
    here, up, down, far = me.x, me.along_x(1), me.along_x(3), me.along_x(2)
    f32 = jnp.float32

    for i in range(blocks):
        at = pl.ds(i * rows, rows)
        for which in range(CORES):
            both = rows_ref[i, me.c if which == 0 else 1 - me.c]
            xp[which, at, :] = both[:, :shard]
            gp[which, at, :] = both[:, shard:]

    def copy(j, lane, src, dst, peer):
        return remote(src, dst, send_sem.at[j, lane], recv_sem.at[j, lane], peer)

    def add(ref, more):
        ref[...] = (ref[...].astype(f32) + more.astype(f32)).astype(jnp.bfloat16)

    def products(j, which, dst):
        cols = pl.ds(j * n, n)
        parts = (
            jnp.dot(xp[which], wg_ref[:, cols], preferred_element_type=f32),
            jnp.dot(xp[which], wu_ref[:, cols], preferred_element_type=f32),
            jnp.dot(gp[which], wd_ref[:, cols], preferred_element_type=f32),
        )
        for k, part in enumerate(parts):
            dst[j, :, :, :, k * n : (k + 1) * n] = part.astype(jnp.bfloat16).reshape(
                Z_WAYS, X_WAYS, rows, n
            )

    def to_partner(j):
        return copy(j, 0, away.at[j], arrived.at[j], me.partner())

    def opposite(j):
        if SUM_ORDER[j] == "x":
            return copy(j, 1, held.at[j, 1 - me.zh, here], first.at[j, 4], me.opposite())
        return copy(j, 1, held.at[j, 1 - me.zh], first.at[j, pl.ds(0, X_WAYS)], me.opposite())

    def ring_first(j, lanes=(0, 1, 2, 3)):
        mine = held.at[j, me.zh]
        if SUM_ORDER[j] == "x":
            table = (
                (held.at[j, 0, far], first.at[j, 0]),
                (held.at[j, 1, far], first.at[j, 1]),
                (held.at[j, 1, up], first.at[j, 2]),
                (held.at[j, 0, down], first.at[j, 3]),
            )
        else:
            table = (
                (mine.at[far, low], second.at[j, 2, low]),
                (mine.at[far, high], second.at[j, 2, high]),
                (mine.at[up, high], second.at[j, 0, high]),
                (mine.at[down, low], second.at[j, 1, low]),
            )
        return [copy(j, 2 + i, *table[i], me.ring(1 + 2 * (i % 2))) for i in lanes]

    def ring_second(j):
        if SUM_ORDER[j] == "x":
            return [
                copy(j, 6, held.at[j, 0, up], second.at[j, 0], me.ring(1)),
                copy(j, 7, held.at[j, 1, down], second.at[j, 1], me.ring(3)),
            ]
        mine = held.at[j, me.zh]
        return [
            copy(j, 6, mine.at[up, low], second.at[j, 0, low], me.ring(1)),
            copy(j, 7, mine.at[down, high], second.at[j, 1, high], me.ring(3)),
        ]

    def arrive(copies):
        for one in copies:
            one.wait_recv()

    def start(copies):
        for one in copies:
            one.start()

    def make(j):
        products(j, 1, away)
        to_partner(j).start()
        products(j, 0, held)

    def cores(j):
        arrive([to_partner(j)])
        for z in range(Z_WAYS):
            add(held.at[j, z], arrived[j, z])
        start(ring_first(j) if SUM_ORDER[j] == "x" else [opposite(j)])

    def pass_on(j):
        copies = ring_second(j)
        if SUM_ORDER[j] == "x":
            arrive(ring_first(j, (0,)))
            add(held.at[j, 0, up], first[j, 0])
            copies[0].start()
            arrive(ring_first(j, (1,)))
            add(held.at[j, 1, down], first[j, 1])
            copies[1].start()
        else:
            arrive(ring_first(j, (0,)))
            add(held.at[j, me.zh, up, low], second[j, 2, low])
            copies[0].start()
            arrive(ring_first(j, (1,)))
            add(held.at[j, me.zh, down, high], second[j, 2, high])
            copies[1].start()

    def gather(j):
        if SUM_ORDER[j] == "x":
            arrive(ring_first(j, (2, 3)) + ring_second(j))
            for z, (one, two) in enumerate(((second.at[j, 0], first.at[j, 3]), (second.at[j, 1], first.at[j, 2]))):
                add(held.at[j, z, here], one[...].astype(f32) + two[...].astype(f32))
            start([opposite(j)])
        else:
            arrive([opposite(j)])
            for x in (me.along_x(2), me.along_x(1), me.along_x(3), me.x):
                add(held.at[j, me.zh, x], first[j, x])
            start(ring_first(j))

    def finish(j):
        total = held[j, me.zh, here].astype(f32)
        if SUM_ORDER[j] == "x":
            arrive([opposite(j)])
            total += first[j, 4].astype(f32)
        else:
            arrive(ring_first(j, (2, 3)) + ring_second(j))
            total += second[j, 0].astype(f32) + second[j, 1].astype(f32)
        weight = pw_ref[...]
        gate, upper, back = total[:, :n], total[:, n : 2 * n], total[:, 2 * n :] * weight
        s = 1.0 / (1.0 + jnp.exp(-gate))
        out_ref[j, :, :n] = (back * upper * s * (1.0 + gate * (1.0 - s))).astype(jnp.bfloat16)
        out_ref[j, :, n:] = (back * gate * s).astype(jnp.bfloat16)
        at = (j % 2) * n
        out_ref[CHUNKS + j // 2, :, at : at + n] = (weight * gate * s * upper).astype(jnp.bfloat16)

    def middle(j, step):
        order = (pass_on, gather) if SUM_ORDER[j] == "x" else (gather, pass_on)
        order[step](j)

    stages = (make, cores, lambda j: middle(j, 0), lambda j: middle(j, 1), finish)
    for t in range(CHUNKS + SUM_LAGS[-1]):
        for stage, lag in zip(stages, SUM_LAGS):
            if 0 <= t - lag < CHUNKS:
                stage(t - lag)
    for j in range(CHUNKS):
        for one in [to_partner(j), opposite(j)] + ring_first(j) + ring_second(j):
            one.wait_send()


def vmem(count):
    return [pl.BlockSpec(memory_space=pltpu.VMEM)] * count


def summed_rows(packed, w_gate, w_up, w_down, weight):
    (blocks, cores, rows, _), (shard, hidden) = packed.shape, w_gate.shape
    cols = 3 * hidden // CHUNKS
    bf16 = jnp.bfloat16
    return pl.pallas_call(
        sum_kernel,
        out_shape=jax.ShapeDtypeStruct((CHUNKS * 3 // 2, rows, 2 * hidden // CHUNKS), bf16),
        in_specs=vmem(5),
        out_specs=vmem(1)[0],
        scratch_shapes=[
            pltpu.VMEM((cores, blocks * rows, shard), bf16),
            pltpu.VMEM((cores, blocks * rows, shard), bf16),
            pltpu.VMEM((CHUNKS, Z_WAYS, X_WAYS, rows, cols), bf16),
            pltpu.VMEM((CHUNKS, Z_WAYS, X_WAYS, rows, cols), bf16),
            pltpu.VMEM((CHUNKS, Z_WAYS, X_WAYS, rows, cols), bf16),
            pltpu.VMEM((CHUNKS, X_WAYS + 1, rows, cols), bf16),
            pltpu.VMEM((CHUNKS, X_WAYS - 1, rows, cols), bf16),
            pltpu.SemaphoreType.DMA((CHUNKS, 8)),
            pltpu.SemaphoreType.DMA((CHUNKS, 8)),
        ],
        compiler_params=pltpu.CompilerParams(
            collective_id=0, has_side_effects=True, vmem_limit_bytes=50 << 20
        ),
    )(packed, w_gate, w_up, w_down, weight)


Y_WAYS, PAIR = 4, 2


class Wide(Place):
    def __init__(self):
        super().__init__()
        self.d = (self.zh * X_WAYS + self.x) * CORES + self.c
        self.y, self.zl = self.expert % Y_WAYS, self.expert // Y_WAYS

    def along_y(self, k):
        return (self.y + k) % Y_WAYS

    def column(self, k):
        return (self.zl * Y_WAYS + self.along_y(k), self.d)

    def holder(self, pair, y_from, core):
        return (pair * Y_WAYS + self.y, (self.zl * X_WAYS + y_from) * CORES + core)

    def source(self, d):
        return (self.zh * Y_WAYS + self.y, d)

    def unless_self(self, peer, act):
        @pl.when((peer[0] != self.expert) | (peer[1] != self.d))
        def _():
            act()

    def greet(self, senders, others):
        barrier = pltpu.get_barrier_semaphore()
        peers = [self.column(k) for k in range(1, Y_WAYS)] + others
        for peer in peers:
            pl.semaphore_signal(barrier, inc=1, device_id=peer, device_id_type=MESH)
        for peer in senders:
            self.unless_self(
                peer,
                lambda peer=peer: pl.semaphore_signal(
                    barrier, inc=1, device_id=peer, device_id_type=MESH
                ),
            )
        pl.semaphore_wait(barrier, len(peers) + len(senders) - jnp.where(self.zl == self.zh, 1, 0))

    def holders(self):
        return [
            self.holder(p, y, core) for p in range(PAIR) for y in range(Y_WAYS) for core in range(CORES)
        ]

    def sources(self):
        return [self.source(d) for d in range(Z_WAYS * X_WAYS * CORES)]


def dispatch_kernel(
    pick_ref, x_ref, g_ref, out_ref, tok, away, mid, send1, recv1, send2, recv2
):
    me = Wide()
    shard = x_ref.shape[1] // CORES
    for h in range(CORES):
        cols = slice(h * shard, (h + 1) * shard)
        tok[h] = jnp.concatenate([x_ref[:, cols], g_ref[:, cols]], axis=1)
    me.greet(me.sources(), [])
    pieces = [(q, h) for h in range(CORES) for q in range(PAIR)]

    def pair(q):
        return (1 - me.zh + q) % PAIR

    def picked(q, h, y):
        rows = jnp.dot(pick_ref[pair(q) * Y_WAYS + y], tok[h], preferred_element_type=jnp.float32)
        return rows.astype(jnp.bfloat16)

    def to_row(q, h, k):
        return remote(
            away.at[h, me.along_y(k), pair(q)], mid.at[h, me.y, pair(q)],
            send1.at[q, h, k - 1], recv1.at[q, h, me.y], me.column(k),
        )

    def to_holder(q, h, k):
        y = me.along_y(k)
        return remote(
            mid.at[h, y, pair(q)], out_ref.at[me.d // CORES, me.c],
            send2.at[q, h, k], recv2.at[me.d], me.holder(pair(q), y, h),
        )

    for q, h in pieces:
        for k in (2, 1, 3):
            y = me.along_y(k)
            away[h, y, pair(q)] = picked(q, h, y)
            to_row(q, h, k).start()
        mid[h, me.y, pair(q)] = picked(q, h, me.y)

    for q, h in pieces:
        for k in (0, 1, 3, 2):
            y = me.along_y(k)
            if k:
                remote(
                    away.at[h, y, pair(q)], mid.at[h, y, pair(q)],
                    send1.at[q, h, 0], recv1.at[q, h, y], me.column(k),
                ).wait_recv()
            peer = me.holder(pair(q), y, h)
            me.unless_self(peer, lambda q=q, h=h, k=k: to_holder(q, h, k).start())

            @pl.when((peer[0] == me.expert) & (peer[1] == me.d))
            def _():
                out_ref[me.d // CORES, me.c] = mid[h, y, pair(q)]

    def from_source(d):
        remote(
            mid.at[0, 0, 0], out_ref.at[d // CORES, d % CORES], send2.at[0, 0, 0], recv2.at[d], me.source(d)
        ).wait_recv()

    for d in range(Z_WAYS * X_WAYS * CORES):
        me.unless_self(me.source(d), lambda d=d: from_source(d))
    for q, h in pieces:
        for k in range(1, Y_WAYS):
            to_row(q, h, k).wait_send()
        for k in range(Y_WAYS):
            me.unless_self(
                me.holder(pair(q), me.along_y(k), h), lambda q=q, h=h, k=k: to_holder(q, h, k).wait_send()
            )


def spread_kernel(
    inv_root, act_ref, rows_ref, wg_ref, wu_ref, low_ref, high_ref, gg_ref, gu_ref, gd_ref, out_ref,
    xt, gt, whole, total, dx, mid, back, send_sem, recv_sem, send1, recv1, send2, recv2,
):
    me = Wide()
    me.greet(me.holders(), [me.partner(), me.opposite(), me.ring(1), me.ring(3)])
    n = wg_ref.shape[1] // CHUNKS
    blocks, rows, shard = X_WAYS * Z_WAYS, rows_ref.shape[2], wg_ref.shape[0]
    slots = CORES * blocks * rows
    low, high = pl.ds(0, rows // 2), pl.ds(rows // 2, rows // 2)
    here, up, down = me.x, me.along_x(1), me.along_x(3)
    f32 = jnp.float32
    spread_chunks = len(SPREAD_ORDER)

    def copy(j, lane, src, dst, peer):
        return remote(src, dst, send_sem.at[j, lane], recv_sem.at[j, lane], peer)

    def part(j, x, half=None):
        if half is None:
            return whole.at[j, 0, me.zh, x] if SPREAD_ORDER[j] == "x" else whole.at[j, 0, :, x]
        return whole.at[j, 0, me.zh, x, half] if SPREAD_ORDER[j] == "x" else whole.at[j, 0, :, x, half]

    def neighbours(j):
        src = act_ref.at[j] if SPREAD_ORDER[j] == "x" else part(j, here)
        return [copy(j, 2, src, part(j, here), me.ring(1)), copy(j, 3, src, part(j, here), me.ring(3))]

    def passed(j):
        return [
            copy(j, 4, part(j, down, low), part(j, down, low), me.ring(1)),
            copy(j, 5, part(j, up, high), part(j, up, high), me.ring(3)),
        ]

    def opposite(j):
        if SPREAD_ORDER[j] == "x":
            return copy(j, 1, whole.at[j, 0, me.zh], whole.at[j, 0, me.zh], me.opposite())
        return copy(j, 1, act_ref.at[j], whole.at[j, 0, me.zh, here], me.opposite())

    def to_partner(j):
        return copy(j, 0, whole.at[j, 0], whole.at[j, 1], me.partner())

    def begin(j):
        if SPREAD_ORDER[j] == "x":
            for one in neighbours(j):
                one.start()
        else:
            opposite(j).start()
        whole[j, 0, me.zh, here] = act_ref[j]

    def relay(j):
        for one, on in zip(neighbours(j), passed(j)):
            one.wait_recv()
            on.start()

    def middle(j, step):
        if SPREAD_ORDER[j] == "x":
            if step == 0:
                relay(j)
            else:
                for one in passed(j):
                    one.wait_recv()
                opposite(j).start()
        elif step == 0:
            opposite(j).wait_recv()
            for one in neighbours(j):
                one.start()
        else:
            relay(j)

    def cores(j):
        if SPREAD_ORDER[j] == "x":
            opposite(j).wait_recv()
        else:
            for one in passed(j):
                one.wait_recv()
        to_partner(j).start()

    def grad(turned, j, cols):
        both = whole[j, :, :, :, :, cols].reshape(slots, -1)
        return (jnp.dot(turned[...], both, preferred_element_type=f32) * inv_root).astype(jnp.bfloat16)

    def inputs(j):
        to_partner(j).wait_recv()
        cols = pl.ds(j * n, n)
        d_gate = whole[j, :, :, :, :, :n].reshape(slots, n)
        d_up = whole[j, :, :, :, :, n:].reshape(slots, n)
        more = lax.dot_general(d_gate, wg_ref[:, cols], LAST, preferred_element_type=f32)
        more += lax.dot_general(d_up, wu_ref[:, cols], LAST, preferred_element_type=f32)
        total[...] = more if j == 0 else total[...] + more

    def weights(j):
        if j < CHUNKS:
            cols = pl.ds(j * n, n)
            gg_ref[:, cols] = grad(xt, j, slice(0, n))
            gu_ref[:, cols] = grad(xt, j, slice(n, 2 * n))
        else:
            to_partner(j).wait_recv()
            gd_ref[:, pl.ds((j - CHUNKS) * 2 * n, 2 * n)] = grad(gt, j, slice(0, 2 * n))

    def to_source(d):
        return remote(
            dx.at[d // CORES, d % CORES], mid.at[me.x, me.zl, me.c], send1.at[d],
            recv1.at[me.x, me.zl, me.c], me.source(d),
        )

    def to_column(k):
        y = me.along_y(k)
        return remote(mid.at[y], back.at[me.y], send2.at[k - 1], recv2.at[me.y], me.column(k))

    def home_first():
        for i in range(blocks):
            for which in range(CORES):
                at = (which * blocks + i) * rows
                one = total[at : at + rows // 2, :].astype(jnp.bfloat16)
                two = total[at + rows // 2 : at + rows, :].astype(jnp.bfloat16)
                dx[i, me.c if which == 0 else 1 - me.c] = jnp.concatenate([one, two], axis=1)
        for k in range(Z_WAYS * X_WAYS * CORES):
            d = (me.d + k + 4) % (Z_WAYS * X_WAYS * CORES)
            me.unless_self(me.source(d), lambda d=d: to_source(d).start())

        @pl.when(me.zl == me.zh)
        def _():
            mid[me.x, me.zl, me.c] = dx[me.d // CORES, me.c]

    def from_holder(p, y, core):
        peer = me.holder(p, y, core)

        def wait():
            remote(
                dx.at[0, 0], mid.at[y, p, core], send1.at[0], recv1.at[y, p, core], peer
            ).wait_recv()

        me.unless_self(peer, wait)

    def home_second():
        for k in (2, 1, 3, 0):
            y = me.along_y(k)
            for p in range(PAIR):
                for core in range(CORES):
                    from_holder(p, y, core)
            if k:
                to_column(k).start()
        back[me.y] = mid[me.y]

    def home():
        for k in range(1, Y_WAYS):
            y = me.along_y(k)
            remote(mid.at[0], back.at[y], send2.at[0], recv2.at[y], me.column(k)).wait_recv()
        parts = []
        for h in range(CORES):
            blocks_of = back[:, :, h].reshape(low_ref.shape[1], CORES * shard)
            one = jnp.dot(low_ref[...], blocks_of, preferred_element_type=f32)
            two = jnp.dot(high_ref[...], blocks_of, preferred_element_type=f32)
            parts.append(one[:, :shard] + two[:, shard:])
        out_ref[...] = jnp.concatenate(parts, axis=1).astype(jnp.bfloat16)

    for j in range(CHUNKS):
        begin(j)
    for lo, turned in ((0, xt), (shard, gt)):
        for i in range(blocks):
            for which in range(CORES):
                at = pl.ds((which * blocks + i) * rows, rows)
                c = me.c if which == 0 else 1 - me.c
                total[at, :] = rows_ref[i, c][:, lo : lo + shard].astype(f32)
        turned[...] = total[...].T.astype(jnp.bfloat16)

    def products(j):
        inputs(j)
        if j == CHUNKS - 1:
            home_first()
        weights(j)

    late = range(CHUNKS, spread_chunks)
    stages = (lambda j: middle(j, 0), lambda j: middle(j, 1), cores, products)
    for t in range(CHUNKS + SPREAD_LAGS[-1]):
        for stage, lag in zip(stages, SPREAD_LAGS):
            if 0 <= t - lag < CHUNKS:
                stage(t - lag)
        if t - LATE_LAG in range(spread_chunks - CHUNKS):
            begin(CHUNKS + t - LATE_LAG)
    for stage in (stages[0], stages[1]):
        for j in late:
            stage(j)
    home_second()
    for stage in (cores, weights):
        for j in late:
            stage(j)
    home()
    for j in range(spread_chunks):
        for one in [to_partner(j), opposite(j)] + neighbours(j) + passed(j):
            one.wait_send()
    for d in range(Z_WAYS * X_WAYS * CORES):
        me.unless_self(me.source(d), lambda d=d: to_source(d).wait_send())
    for k in range(1, Y_WAYS):
        to_column(k).wait_send()


def dispatched(pick, x, g):
    (_, rows, _), (tokens, width) = pick.shape, x.shape
    bf16 = jnp.bfloat16
    groups = X_WAYS * Z_WAYS
    dma = pltpu.SemaphoreType.DMA
    return pl.pallas_call(
        dispatch_kernel,
        out_shape=jax.ShapeDtypeStruct((groups, CORES, rows, width), bf16),
        in_specs=vmem(3),
        out_specs=vmem(1)[0],
        scratch_shapes=[
            pltpu.VMEM((CORES, tokens, width), bf16),
            pltpu.VMEM((CORES, Y_WAYS, PAIR, rows, width), bf16),
            pltpu.VMEM((CORES, Y_WAYS, PAIR, rows, width), bf16),
            dma((PAIR, CORES, Y_WAYS - 1)),
            dma((PAIR, CORES, Y_WAYS)),
            dma((PAIR, CORES, Y_WAYS)),
            dma((groups * CORES,)),
        ],
        compiler_params=pltpu.CompilerParams(
            collective_id=2, has_side_effects=True, vmem_limit_bytes=20 << 20
        ),
    )(pick, x, g)


def spread_rows(inv_root, act, packed, w_gate, w_up, low, high):
    (blocks, cores, rows, width), (shard, hidden) = packed.shape, w_gate.shape
    cols = 2 * hidden // CHUNKS
    slots = cores * blocks * rows
    count = len(SPREAD_ORDER)
    bf16, dma = jnp.bfloat16, pltpu.SemaphoreType.DMA
    return pl.pallas_call(
        functools.partial(spread_kernel, inv_root),
        out_shape=(
            jax.ShapeDtypeStruct((shard, hidden), bf16),
            jax.ShapeDtypeStruct((shard, hidden), bf16),
            jax.ShapeDtypeStruct((shard, hidden), bf16),
            jax.ShapeDtypeStruct((low.shape[0], width), bf16),
        ),
        in_specs=vmem(6),
        out_specs=vmem(4),
        scratch_shapes=[
            pltpu.VMEM((shard, slots), bf16),
            pltpu.VMEM((shard, slots), bf16),
            pltpu.VMEM((count, cores, Z_WAYS, X_WAYS, rows, cols), bf16),
            pltpu.VMEM((slots, shard), jnp.float32),
            pltpu.VMEM((blocks, cores, rows // 2, width), bf16),
            pltpu.VMEM((Y_WAYS, PAIR, cores, rows // 2, width), bf16),
            pltpu.VMEM((Y_WAYS, PAIR, cores, rows // 2, width), bf16),
            dma((count, 6)),
            dma((count, 6)),
            dma((blocks * cores,)),
            dma((Y_WAYS, PAIR, cores)),
            dma((Y_WAYS - 1,)),
            dma((Y_WAYS,)),
        ],
        compiler_params=pltpu.CompilerParams(
            collective_id=1, has_side_effects=True, vmem_limit_bytes=50 << 20
        ),
    )(act, packed, w_gate, w_up, low, high)


def body(tokens, grad_out, expert_ids, route_weights, w_gate, w_up, w_down):
    experts = lax.axis_size("expert")
    groups = lax.axis_size("dp")
    tok_rows = tokens.shape[0]
    capacity = tok_rows // 2
    expert_index = lax.axis_index("expert")
    inv_root = 1.0 / math.sqrt(tok_rows * groups)
    gate_shard, up_shard, down_shard = w_gate[0], w_up[0], w_down[0].T

    names = jnp.arange(experts, dtype=jnp.int32)[:, None]
    hit0 = expert_ids[:, 0][None, :] == names
    hit1 = expert_ids[:, 1][None, :] == names
    hit = (hit0 | hit1).astype(jnp.bfloat16)
    index = jnp.arange(tok_rows, dtype=jnp.int32)
    before = (index[:, None] < index[None, :]).astype(jnp.bfloat16)
    rank = jnp.dot(hit, before, preferred_element_type=jnp.float32)
    rank = jnp.where(hit > 0, rank, -1.0).astype(jnp.int32)
    chosen = rank[:, None, :] == jnp.arange(capacity, dtype=jnp.int32)[None, :, None]
    pick = chosen.astype(jnp.bfloat16)

    def place(first):
        by_row = rank.reshape(PAIR, Y_WAYS, tok_rows).transpose(2, 1, 0).reshape(tok_rows, experts)
        part = by_row[:, :, None] == jnp.arange(first, first + capacity // 2, dtype=jnp.int32)
        return part.astype(jnp.bfloat16).reshape(tok_rows, experts * capacity // 2)

    weight_of = jnp.where(hit0, route_weights[:, 0][None, :], 0.0) + jnp.where(
        hit1, route_weights[:, 1][None, :], 0.0
    )
    own_rank = lax.dynamic_slice_in_dim(rank, expert_index, 1)
    own_weight_of = lax.dynamic_slice_in_dim(weight_of, expert_index, 1)
    own_weight = jnp.sum(
        jnp.where(
            own_rank == jnp.arange(capacity, dtype=jnp.int32)[:, None], own_weight_of, 0.0
        ),
        axis=1,
    )

    packed = dispatched(pick, tokens, grad_out)
    act = summed_rows(packed, gate_shard, up_shard, down_shard, own_weight[:, None])
    grad_g, grad_u, grad_d, grad_tokens = spread_rows(
        inv_root, act, packed, gate_shard, up_shard, place(0), place(capacity // 2)
    )
    return (grad_tokens, grad_g[None], grad_u[None], grad_d.T[None])


def solution(mesh):
    in_specs = (
        P("dp", "expert"),
        P("dp", "expert"),
        P("dp", None),
        P("dp", None),
        P("expert", "dp", None),
        P("expert", "dp", None),
        P("expert", None, "dp"),
    )
    out_specs = (
        P("dp", "expert"),
        P("expert", "dp", None),
        P("expert", "dp", None),
        P("expert", None, "dp"),
    )
    return jax.shard_map(body, mesh=mesh, in_specs=in_specs, out_specs=out_specs, check_vma=False)
```

```python
import functools
import math

import jax
import jax.numpy as jnp
from jax import lax
from jax.experimental import pallas as pl
from jax.experimental.pallas import tpu as pltpu
from jax.sharding import PartitionSpec as P

MESH = pl.DeviceIdType.MESH
CHUNKS = 8
X_WAYS, Z_WAYS, CORES = 4, 2, 2
LAST = (((1,), (1,)), ((), ()))
SUM_ORDER = "xzxzxxzx"
SPREAD_ORDER = "xzxzzxzzzzzx"
SUM_LAGS = (0, 1, 5, 7, 9)
SPREAD_LAGS = (0, 2, 4, 5)
LATE_LAG = 8


class Place:
    def __init__(self):
        self.expert = lax.axis_index("expert")
        d = lax.axis_index("dp")
        self.c = d % CORES
        self.x = (d // CORES) % X_WAYS
        self.zh = d // (CORES * X_WAYS)

    def at(self, zh, x, c):
        return (self.expert, (zh * X_WAYS + x) * CORES + c)

    def partner(self):
        return self.at(self.zh, self.x, 1 - self.c)

    def opposite(self):
        return self.at(1 - self.zh, self.x, self.c)

    def along_x(self, k):
        return (self.x + k) % X_WAYS

    def ring(self, k):
        return self.at(self.zh, self.along_x(k), self.c)

    def greet(self):
        barrier = pltpu.get_barrier_semaphore()
        peers = [self.partner(), self.opposite(), self.ring(1), self.ring(3)]
        for peer in peers:
            pl.semaphore_signal(barrier, inc=1, device_id=peer, device_id_type=MESH)
        pl.semaphore_wait(barrier, len(peers))


def remote(src, dst, send_sem, recv_sem, peer):
    return pltpu.make_async_remote_copy(
        src_ref=src, dst_ref=dst, send_sem=send_sem, recv_sem=recv_sem,
        device_id=peer, device_id_type=MESH,
    )


def sum_kernel(
    rows_ref, wg_ref, wu_ref, wd_ref, pw_ref, out_ref,
    xp, gp, away, arrived, held, first, second, send_sem, recv_sem,
):
    me = Place()
    me.greet()
    n = wg_ref.shape[1] // CHUNKS
    blocks, rows, shard = X_WAYS * Z_WAYS, rows_ref.shape[2], wg_ref.shape[0]
    low, high = pl.ds(0, rows // 2), pl.ds(rows // 2, rows // 2)
    here, up, down, far = me.x, me.along_x(1), me.along_x(3), me.along_x(2)
    f32 = jnp.float32

    for i in range(blocks):
        at = pl.ds(i * rows, rows)
        for which in range(CORES):
            both = rows_ref[i, me.c if which == 0 else 1 - me.c]
            xp[which, at, :] = both[:, :shard]
            gp[which, at, :] = both[:, shard:]

    def copy(j, lane, src, dst, peer):
        return remote(src, dst, send_sem.at[j, lane], recv_sem.at[j, lane], peer)

    def add(ref, more):
        ref[...] = (ref[...].astype(f32) + more.astype(f32)).astype(jnp.bfloat16)

    def products(j, which, dst):
        cols = pl.ds(j * n, n)
        parts = (
            jnp.dot(xp[which], wg_ref[:, cols], preferred_element_type=f32),
            jnp.dot(xp[which], wu_ref[:, cols], preferred_element_type=f32),
            jnp.dot(gp[which], wd_ref[:, cols], preferred_element_type=f32),
        )
        for k, part in enumerate(parts):
            dst[j, :, :, :, k * n : (k + 1) * n] = part.astype(jnp.bfloat16).reshape(
                Z_WAYS, X_WAYS, rows, n
            )

    def to_partner(j):
        return copy(j, 0, away.at[j], arrived.at[j], me.partner())

    def opposite(j):
        if SUM_ORDER[j] == "x":
            return copy(j, 1, held.at[j, 1 - me.zh, here], first.at[j, 4], me.opposite())
        return copy(j, 1, held.at[j, 1 - me.zh], first.at[j, pl.ds(0, X_WAYS)], me.opposite())

    def ring_first(j, lanes=(0, 1, 2, 3)):
        mine = held.at[j, me.zh]
        if SUM_ORDER[j] == "x":
            table = (
                (held.at[j, 0, far], first.at[j, 0]),
                (held.at[j, 1, far], first.at[j, 1]),
                (held.at[j, 1, up], first.at[j, 2]),
                (held.at[j, 0, down], first.at[j, 3]),
            )
        else:
            table = (
                (mine.at[far, low], second.at[j, 2, low]),
                (mine.at[far, high], second.at[j, 2, high]),
                (mine.at[up, high], second.at[j, 0, high]),
                (mine.at[down, low], second.at[j, 1, low]),
            )
        return [copy(j, 2 + i, *table[i], me.ring(1 + 2 * (i % 2))) for i in lanes]

    def ring_second(j):
        if SUM_ORDER[j] == "x":
            return [
                copy(j, 6, held.at[j, 0, up], second.at[j, 0], me.ring(1)),
                copy(j, 7, held.at[j, 1, down], second.at[j, 1], me.ring(3)),
            ]
        mine = held.at[j, me.zh]
        return [
            copy(j, 6, mine.at[up, low], second.at[j, 0, low], me.ring(1)),
            copy(j, 7, mine.at[down, high], second.at[j, 1, high], me.ring(3)),
        ]

    def arrive(copies):
        for one in copies:
            one.wait_recv()

    def start(copies):
        for one in copies:
            one.start()

    def make(j):
        products(j, 1, away)
        to_partner(j).start()
        products(j, 0, held)

    def cores(j):
        arrive([to_partner(j)])
        for z in range(Z_WAYS):
            add(held.at[j, z], arrived[j, z])
        start(ring_first(j) if SUM_ORDER[j] == "x" else [opposite(j)])

    def pass_on(j):
        copies = ring_second(j)
        if SUM_ORDER[j] == "x":
            arrive(ring_first(j, (0,)))
            add(held.at[j, 0, up], first[j, 0])
            copies[0].start()
            arrive(ring_first(j, (1,)))
            add(held.at[j, 1, down], first[j, 1])
            copies[1].start()
        else:
            arrive(ring_first(j, (0,)))
            add(held.at[j, me.zh, up, low], second[j, 2, low])
            copies[0].start()
            arrive(ring_first(j, (1,)))
            add(held.at[j, me.zh, down, high], second[j, 2, high])
            copies[1].start()

    def gather(j):
        if SUM_ORDER[j] == "x":
            arrive(ring_first(j, (2, 3)) + ring_second(j))
            for z, (one, two) in enumerate(((second.at[j, 0], first.at[j, 3]), (second.at[j, 1], first.at[j, 2]))):
                add(held.at[j, z, here], one[...].astype(f32) + two[...].astype(f32))
            start([opposite(j)])
        else:
            arrive([opposite(j)])
            for x in (me.along_x(2), me.along_x(1), me.along_x(3), me.x):
                add(held.at[j, me.zh, x], first[j, x])
            start(ring_first(j))

    def finish(j):
        total = held[j, me.zh, here].astype(f32)
        if SUM_ORDER[j] == "x":
            arrive([opposite(j)])
            total += first[j, 4].astype(f32)
        else:
            arrive(ring_first(j, (2, 3)) + ring_second(j))
            total += second[j, 0].astype(f32) + second[j, 1].astype(f32)
        weight = pw_ref[...]
        gate, upper, back = total[:, :n], total[:, n : 2 * n], total[:, 2 * n :] * weight
        s = 1.0 / (1.0 + jnp.exp(-gate))
        out_ref[j, :, :n] = (back * upper * s * (1.0 + gate * (1.0 - s))).astype(jnp.bfloat16)
        out_ref[j, :, n:] = (back * gate * s).astype(jnp.bfloat16)
        at = (j % 2) * n
        out_ref[CHUNKS + j // 2, :, at : at + n] = (weight * gate * s * upper).astype(jnp.bfloat16)

    def middle(j, step):
        order = (pass_on, gather) if SUM_ORDER[j] == "x" else (gather, pass_on)
        order[step](j)

    stages = (make, cores, lambda j: middle(j, 0), lambda j: middle(j, 1), finish)
    for t in range(CHUNKS + SUM_LAGS[-1]):
        for stage, lag in zip(stages, SUM_LAGS):
            if 0 <= t - lag < CHUNKS:
                stage(t - lag)
    for j in range(CHUNKS):
        for one in [to_partner(j), opposite(j)] + ring_first(j) + ring_second(j):
            one.wait_send()


def vmem(count):
    return [pl.BlockSpec(memory_space=pltpu.VMEM)] * count


def summed_rows(packed, w_gate, w_up, w_down, weight):
    (blocks, cores, rows, _), (shard, hidden) = packed.shape, w_gate.shape
    cols = 3 * hidden // CHUNKS
    bf16 = jnp.bfloat16
    return pl.pallas_call(
        sum_kernel,
        out_shape=jax.ShapeDtypeStruct((CHUNKS * 3 // 2, rows, 2 * hidden // CHUNKS), bf16),
        in_specs=vmem(5),
        out_specs=vmem(1)[0],
        scratch_shapes=[
            pltpu.VMEM((cores, blocks * rows, shard), bf16),
            pltpu.VMEM((cores, blocks * rows, shard), bf16),
            pltpu.VMEM((CHUNKS, Z_WAYS, X_WAYS, rows, cols), bf16),
            pltpu.VMEM((CHUNKS, Z_WAYS, X_WAYS, rows, cols), bf16),
            pltpu.VMEM((CHUNKS, Z_WAYS, X_WAYS, rows, cols), bf16),
            pltpu.VMEM((CHUNKS, X_WAYS + 1, rows, cols), bf16),
            pltpu.VMEM((CHUNKS, X_WAYS - 1, rows, cols), bf16),
            pltpu.SemaphoreType.DMA((CHUNKS, 8)),
            pltpu.SemaphoreType.DMA((CHUNKS, 8)),
        ],
        compiler_params=pltpu.CompilerParams(
            collective_id=0, has_side_effects=True, vmem_limit_bytes=50 << 20
        ),
    )(packed, w_gate, w_up, w_down, weight)


Y_WAYS, PAIR = 4, 2


class Wide(Place):
    def __init__(self):
        super().__init__()
        self.d = (self.zh * X_WAYS + self.x) * CORES + self.c
        self.y, self.zl = self.expert % Y_WAYS, self.expert // Y_WAYS

    def along_y(self, k):
        return (self.y + k) % Y_WAYS

    def column(self, k):
        return (self.zl * Y_WAYS + self.along_y(k), self.d)

    def holder(self, pair, y_from, core):
        return (pair * Y_WAYS + self.y, (self.zl * X_WAYS + y_from) * CORES + core)

    def source(self, d):
        return (self.zh * Y_WAYS + self.y, d)

    def unless_self(self, peer, act):
        @pl.when((peer[0] != self.expert) | (peer[1] != self.d))
        def _():
            act()

    def greet(self, senders, others):
        barrier = pltpu.get_barrier_semaphore()
        peers = [self.column(k) for k in range(1, Y_WAYS)] + others
        for peer in peers:
            pl.semaphore_signal(barrier, inc=1, device_id=peer, device_id_type=MESH)
        for peer in senders:
            self.unless_self(
                peer,
                lambda peer=peer: pl.semaphore_signal(
                    barrier, inc=1, device_id=peer, device_id_type=MESH
                ),
            )
        pl.semaphore_wait(barrier, len(peers) + len(senders) - jnp.where(self.zl == self.zh, 1, 0))

    def holders(self):
        return [
            self.holder(p, y, core) for p in range(PAIR) for y in range(Y_WAYS) for core in range(CORES)
        ]

    def sources(self):
        return [self.source(d) for d in range(Z_WAYS * X_WAYS * CORES)]


def dispatch_kernel(
    pick_ref, x_ref, g_ref, out_ref, tok, away, mid, send1, recv1, send2, recv2
):
    me = Wide()
    shard = x_ref.shape[1] // CORES
    for h in range(CORES):
        cols = slice(h * shard, (h + 1) * shard)
        tok[h] = jnp.concatenate([x_ref[:, cols], g_ref[:, cols]], axis=1)
    me.greet(me.sources(), [])
    pieces = [(q, h) for h in range(CORES) for q in range(PAIR)]

    def pair(q):
        return (1 - me.zh + q) % PAIR

    def picked(q, h, y):
        rows = jnp.dot(pick_ref[pair(q) * Y_WAYS + y], tok[h], preferred_element_type=jnp.float32)
        return rows.astype(jnp.bfloat16)

    def to_row(q, h, k):
        return remote(
            away.at[h, me.along_y(k), pair(q)], mid.at[h, me.y, pair(q)],
            send1.at[q, h, k - 1], recv1.at[q, h, me.y], me.column(k),
        )

    def to_holder(q, h, k):
        y = me.along_y(k)
        return remote(
            mid.at[h, y, pair(q)], out_ref.at[me.d // CORES, me.c],
            send2.at[q, h, k], recv2.at[me.d], me.holder(pair(q), y, h),
        )

    for q, h in pieces:
        for k in (2, 1, 3):
            y = me.along_y(k)
            away[h, y, pair(q)] = picked(q, h, y)
            to_row(q, h, k).start()
        mid[h, me.y, pair(q)] = picked(q, h, me.y)

    for q, h in pieces:
        for k in (0, 1, 3, 2):
            y = me.along_y(k)
            if k:
                remote(
                    away.at[h, y, pair(q)], mid.at[h, y, pair(q)],
                    send1.at[q, h, 0], recv1.at[q, h, y], me.column(k),
                ).wait_recv()
            peer = me.holder(pair(q), y, h)
            me.unless_self(peer, lambda q=q, h=h, k=k: to_holder(q, h, k).start())

            @pl.when((peer[0] == me.expert) & (peer[1] == me.d))
            def _():
                out_ref[me.d // CORES, me.c] = mid[h, y, pair(q)]

    def from_source(d):
        remote(
            mid.at[0, 0, 0], out_ref.at[d // CORES, d % CORES], send2.at[0, 0, 0], recv2.at[d], me.source(d)
        ).wait_recv()

    for d in range(Z_WAYS * X_WAYS * CORES):
        me.unless_self(me.source(d), lambda d=d: from_source(d))
    for q, h in pieces:
        for k in range(1, Y_WAYS):
            to_row(q, h, k).wait_send()
        for k in range(Y_WAYS):
            me.unless_self(
                me.holder(pair(q), me.along_y(k), h), lambda q=q, h=h, k=k: to_holder(q, h, k).wait_send()
            )


def spread_kernel(
    inv_root, act_ref, rows_ref, wg_ref, wu_ref, low_ref, high_ref, gg_ref, gu_ref, gd_ref, out_ref,
    xt, gt, whole, total, dx, mid, back, send_sem, recv_sem, send1, recv1, send2, recv2,
):
    me = Wide()
    me.greet(me.holders(), [me.partner(), me.opposite(), me.ring(1), me.ring(3)])
    n = wg_ref.shape[1] // CHUNKS
    blocks, rows, shard = X_WAYS * Z_WAYS, rows_ref.shape[2], wg_ref.shape[0]
    slots = CORES * blocks * rows
    low, high = pl.ds(0, rows // 2), pl.ds(rows // 2, rows // 2)
    here, up, down = me.x, me.along_x(1), me.along_x(3)
    f32 = jnp.float32
    spread_chunks = len(SPREAD_ORDER)

    def copy(j, lane, src, dst, peer):
        return remote(src, dst, send_sem.at[j, lane], recv_sem.at[j, lane], peer)

    def part(j, x, half=None):
        if half is None:
            return whole.at[j, 0, me.zh, x] if SPREAD_ORDER[j] == "x" else whole.at[j, 0, :, x]
        return whole.at[j, 0, me.zh, x, half] if SPREAD_ORDER[j] == "x" else whole.at[j, 0, :, x, half]

    def neighbours(j):
        src = act_ref.at[j] if SPREAD_ORDER[j] == "x" else part(j, here)
        return [copy(j, 2, src, part(j, here), me.ring(1)), copy(j, 3, src, part(j, here), me.ring(3))]

    def passed(j):
        return [
            copy(j, 4, part(j, down, low), part(j, down, low), me.ring(1)),
            copy(j, 5, part(j, up, high), part(j, up, high), me.ring(3)),
        ]

    def opposite(j):
        if SPREAD_ORDER[j] == "x":
            return copy(j, 1, whole.at[j, 0, me.zh], whole.at[j, 0, me.zh], me.opposite())
        return copy(j, 1, act_ref.at[j], whole.at[j, 0, me.zh, here], me.opposite())

    def to_partner(j):
        return copy(j, 0, whole.at[j, 0], whole.at[j, 1], me.partner())

    def begin(j):
        if SPREAD_ORDER[j] == "x":
            for one in neighbours(j):
                one.start()
        else:
            opposite(j).start()
        whole[j, 0, me.zh, here] = act_ref[j]

    def relay(j):
        for one, on in zip(neighbours(j), passed(j)):
            one.wait_recv()
            on.start()

    def middle(j, step):
        if SPREAD_ORDER[j] == "x":
            if step == 0:
                relay(j)
            else:
                for one in passed(j):
                    one.wait_recv()
                opposite(j).start()
        elif step == 0:
            opposite(j).wait_recv()
            for one in neighbours(j):
                one.start()
        else:
            relay(j)

    def cores(j):
        if SPREAD_ORDER[j] == "x":
            opposite(j).wait_recv()
        else:
            for one in passed(j):
                one.wait_recv()
        to_partner(j).start()

    def grad(turned, j, cols):
        both = whole[j, :, :, :, :, cols].reshape(slots, -1)
        return (jnp.dot(turned[...], both, preferred_element_type=f32) * inv_root).astype(jnp.bfloat16)

    def inputs(j):
        to_partner(j).wait_recv()
        cols = pl.ds(j * n, n)
        d_gate = whole[j, :, :, :, :, :n].reshape(slots, n)
        d_up = whole[j, :, :, :, :, n:].reshape(slots, n)
        more = lax.dot_general(d_gate, wg_ref[:, cols], LAST, preferred_element_type=f32)
        more += lax.dot_general(d_up, wu_ref[:, cols], LAST, preferred_element_type=f32)
        total[...] = more if j == 0 else total[...] + more

    def weights(j):
        if j < CHUNKS:
            cols = pl.ds(j * n, n)
            gg_ref[:, cols] = grad(xt, j, slice(0, n))
            gu_ref[:, cols] = grad(xt, j, slice(n, 2 * n))
        else:
            to_partner(j).wait_recv()
            gd_ref[:, pl.ds((j - CHUNKS) * 2 * n, 2 * n)] = grad(gt, j, slice(0, 2 * n))

    def to_source(d):
        return remote(
            dx.at[d // CORES, d % CORES], mid.at[me.x, me.zl, me.c], send1.at[d],
            recv1.at[me.x, me.zl, me.c], me.source(d),
        )

    def to_column(k):
        y = me.along_y(k)
        return remote(mid.at[y], back.at[me.y], send2.at[k - 1], recv2.at[me.y], me.column(k))

    def home_first():
        for i in range(blocks):
            for which in range(CORES):
                at = (which * blocks + i) * rows
                one = total[at : at + rows // 2, :].astype(jnp.bfloat16)
                two = total[at + rows // 2 : at + rows, :].astype(jnp.bfloat16)
                dx[i, me.c if which == 0 else 1 - me.c] = jnp.concatenate([one, two], axis=1)
        for k in range(Z_WAYS * X_WAYS * CORES):
            d = (me.d + k + 4) % (Z_WAYS * X_WAYS * CORES)
            me.unless_self(me.source(d), lambda d=d: to_source(d).start())

        @pl.when(me.zl == me.zh)
        def _():
            mid[me.x, me.zl, me.c] = dx[me.d // CORES, me.c]

    def from_holder(p, y, core):
        peer = me.holder(p, y, core)

        def wait():
            remote(
                dx.at[0, 0], mid.at[y, p, core], send1.at[0], recv1.at[y, p, core], peer
            ).wait_recv()

        me.unless_self(peer, wait)

    def home_second():
        for k in (2, 1, 3, 0):
            y = me.along_y(k)
            for p in range(PAIR):
                for core in range(CORES):
                    from_holder(p, y, core)
            if k:
                to_column(k).start()
        back[me.y] = mid[me.y]

    def home():
        for k in range(1, Y_WAYS):
            y = me.along_y(k)
            remote(mid.at[0], back.at[y], send2.at[0], recv2.at[y], me.column(k)).wait_recv()
        parts = []
        for h in range(CORES):
            blocks_of = back[:, :, h].reshape(low_ref.shape[1], CORES * shard)
            one = jnp.dot(low_ref[...], blocks_of, preferred_element_type=f32)
            two = jnp.dot(high_ref[...], blocks_of, preferred_element_type=f32)
            parts.append(one[:, :shard] + two[:, shard:])
        out_ref[...] = jnp.concatenate(parts, axis=1).astype(jnp.bfloat16)

    for j in range(CHUNKS):
        begin(j)
    def turn(turned, lo):
        for i in range(blocks):
            for which in range(CORES):
                at = pl.ds((which * blocks + i) * rows, rows)
                c = me.c if which == 0 else 1 - me.c
                total[at, :] = rows_ref[i, c][:, lo : lo + shard].astype(f32)
        turned[...] = total[...].T.astype(jnp.bfloat16)

    late = range(CHUNKS, spread_chunks)
    stages = (lambda j: middle(j, 0), lambda j: middle(j, 1), cores, inputs)
    for t in range(CHUNKS + SPREAD_LAGS[-1]):
        for stage, lag in zip(stages, SPREAD_LAGS):
            if 0 <= t - lag < CHUNKS:
                stage(t - lag)
        if t - LATE_LAG in range(spread_chunks - CHUNKS):
            begin(CHUNKS + t - LATE_LAG)
    home_first()
    for j in late:
        stages[0](j)
    turn(xt, 0)
    for j in late:
        weights(2 * (j - CHUNKS))
        stages[1](j)
    turn(gt, shard)
    home_second()
    for j in late:
        cores(j)
        weights(2 * (j - CHUNKS) + 1)
    for j in late:
        weights(j)
    home()
    for j in range(spread_chunks):
        for one in [to_partner(j), opposite(j)] + neighbours(j) + passed(j):
            one.wait_send()
    for d in range(Z_WAYS * X_WAYS * CORES):
        me.unless_self(me.source(d), lambda d=d: to_source(d).wait_send())
    for k in range(1, Y_WAYS):
        to_column(k).wait_send()


def dispatched(pick, x, g):
    (_, rows, _), (tokens, width) = pick.shape, x.shape
    bf16 = jnp.bfloat16
    groups = X_WAYS * Z_WAYS
    dma = pltpu.SemaphoreType.DMA
    return pl.pallas_call(
        dispatch_kernel,
        out_shape=jax.ShapeDtypeStruct((groups, CORES, rows, width), bf16),
        in_specs=vmem(3),
        out_specs=vmem(1)[0],
        scratch_shapes=[
            pltpu.VMEM((CORES, tokens, width), bf16),
            pltpu.VMEM((CORES, Y_WAYS, PAIR, rows, width), bf16),
            pltpu.VMEM((CORES, Y_WAYS, PAIR, rows, width), bf16),
            dma((PAIR, CORES, Y_WAYS - 1)),
            dma((PAIR, CORES, Y_WAYS)),
            dma((PAIR, CORES, Y_WAYS)),
            dma((groups * CORES,)),
        ],
        compiler_params=pltpu.CompilerParams(
            collective_id=2, has_side_effects=True, vmem_limit_bytes=20 << 20
        ),
    )(pick, x, g)


def spread_rows(inv_root, act, packed, w_gate, w_up, low, high):
    (blocks, cores, rows, width), (shard, hidden) = packed.shape, w_gate.shape
    cols = 2 * hidden // CHUNKS
    slots = cores * blocks * rows
    count = len(SPREAD_ORDER)
    bf16, dma = jnp.bfloat16, pltpu.SemaphoreType.DMA
    return pl.pallas_call(
        functools.partial(spread_kernel, inv_root),
        out_shape=(
            jax.ShapeDtypeStruct((shard, hidden), bf16),
            jax.ShapeDtypeStruct((shard, hidden), bf16),
            jax.ShapeDtypeStruct((shard, hidden), bf16),
            jax.ShapeDtypeStruct((low.shape[0], width), bf16),
        ),
        in_specs=vmem(6),
        out_specs=vmem(4),
        scratch_shapes=[
            pltpu.VMEM((shard, slots), bf16),
            pltpu.VMEM((shard, slots), bf16),
            pltpu.VMEM((count, cores, Z_WAYS, X_WAYS, rows, cols), bf16),
            pltpu.VMEM((slots, shard), jnp.float32),
            pltpu.VMEM((blocks, cores, rows // 2, width), bf16),
            pltpu.VMEM((Y_WAYS, PAIR, cores, rows // 2, width), bf16),
            pltpu.VMEM((Y_WAYS, PAIR, cores, rows // 2, width), bf16),
            dma((count, 6)),
            dma((count, 6)),
            dma((blocks * cores,)),
            dma((Y_WAYS, PAIR, cores)),
            dma((Y_WAYS - 1,)),
            dma((Y_WAYS,)),
        ],
        compiler_params=pltpu.CompilerParams(
            collective_id=1, has_side_effects=True, vmem_limit_bytes=50 << 20
        ),
    )(act, packed, w_gate, w_up, low, high)


def body(tokens, grad_out, expert_ids, route_weights, w_gate, w_up, w_down):
    experts = lax.axis_size("expert")
    groups = lax.axis_size("dp")
    tok_rows = tokens.shape[0]
    capacity = tok_rows // 2
    expert_index = lax.axis_index("expert")
    inv_root = 1.0 / math.sqrt(tok_rows * groups)
    gate_shard, up_shard, down_shard = w_gate[0], w_up[0], w_down[0].T

    names = jnp.arange(experts, dtype=jnp.int32)[:, None]
    hit0 = expert_ids[:, 0][None, :] == names
    hit1 = expert_ids[:, 1][None, :] == names
    hit = (hit0 | hit1).astype(jnp.bfloat16)
    index = jnp.arange(tok_rows, dtype=jnp.int32)
    before = (index[:, None] < index[None, :]).astype(jnp.bfloat16)
    rank = jnp.dot(hit, before, preferred_element_type=jnp.float32)
    rank = jnp.where(hit > 0, rank, -1.0).astype(jnp.int32)
    chosen = rank[:, None, :] == jnp.arange(capacity, dtype=jnp.int32)[None, :, None]
    pick = chosen.astype(jnp.bfloat16)

    def place(first):
        by_row = rank.reshape(PAIR, Y_WAYS, tok_rows).transpose(2, 1, 0).reshape(tok_rows, experts)
        part = by_row[:, :, None] == jnp.arange(first, first + capacity // 2, dtype=jnp.int32)
        return part.astype(jnp.bfloat16).reshape(tok_rows, experts * capacity // 2)

    weight_of = jnp.where(hit0, route_weights[:, 0][None, :], 0.0) + jnp.where(
        hit1, route_weights[:, 1][None, :], 0.0
    )
    own_rank = lax.dynamic_slice_in_dim(rank, expert_index, 1)
    own_weight_of = lax.dynamic_slice_in_dim(weight_of, expert_index, 1)
    own_weight = jnp.sum(
        jnp.where(
            own_rank == jnp.arange(capacity, dtype=jnp.int32)[:, None], own_weight_of, 0.0
        ),
        axis=1,
    )

    packed = dispatched(pick, tokens, grad_out)
    act = summed_rows(packed, gate_shard, up_shard, down_shard, own_weight[:, None])
    grad_g, grad_u, grad_d, grad_tokens = spread_rows(
        inv_root, act, packed, gate_shard, up_shard, place(0), place(capacity // 2)
    )
    return (grad_tokens, grad_g[None], grad_u[None], grad_d.T[None])


def solution(mesh):
    in_specs = (
        P("dp", "expert"),
        P("dp", "expert"),
        P("dp", None),
        P("dp", None),
        P("expert", "dp", None),
        P("expert", "dp", None),
        P("expert", None, "dp"),
    )
    out_specs = (
        P("dp", "expert"),
        P("expert", "dp", None),
        P("expert", "dp", None),
        P("expert", None, "dp"),
    )
    return jax.shard_map(body, mesh=mesh, in_specs=in_specs, out_specs=out_specs, check_vma=False)
```

```python
import functools
import math

import jax
import jax.numpy as jnp
from jax import lax
from jax.experimental import pallas as pl
from jax.experimental.pallas import tpu as pltpu
from jax.sharding import PartitionSpec as P

MESH = pl.DeviceIdType.MESH
CHUNKS = 8
X_WAYS, Z_WAYS, CORES = 4, 2, 2
LAST = (((1,), (1,)), ((), ()))
SUM_ORDER = "xzxzxxzx"
SPREAD_ORDER = "xzxzzxzzzzzx"
SUM_LAGS = (0, 1, 4, 6, 8)
SPREAD_LAGS = (2, 4, 6, 7)
LATE_LAG = 8


class Place:
    def __init__(self):
        self.expert = lax.axis_index("expert")
        d = lax.axis_index("dp")
        self.c = d % CORES
        self.x = (d // CORES) % X_WAYS
        self.zh = d // (CORES * X_WAYS)

    def at(self, zh, x, c):
        return (self.expert, (zh * X_WAYS + x) * CORES + c)

    def partner(self):
        return self.at(self.zh, self.x, 1 - self.c)

    def opposite(self):
        return self.at(1 - self.zh, self.x, self.c)

    def along_x(self, k):
        return (self.x + k) % X_WAYS

    def ring(self, k):
        return self.at(self.zh, self.along_x(k), self.c)

    def greet(self):
        barrier = pltpu.get_barrier_semaphore()
        peers = [self.partner(), self.opposite(), self.ring(1), self.ring(3)]
        for peer in peers:
            pl.semaphore_signal(barrier, inc=1, device_id=peer, device_id_type=MESH)
        pl.semaphore_wait(barrier, len(peers))


def remote(src, dst, send_sem, recv_sem, peer):
    return pltpu.make_async_remote_copy(
        src_ref=src, dst_ref=dst, send_sem=send_sem, recv_sem=recv_sem,
        device_id=peer, device_id_type=MESH,
    )


def sum_stages(
    me, rows_ref, wg_ref, wu_ref, wd_ref, pw_ref, out_ref,
    xp, gp, away, arrived, held, first, second, send_sem, recv_sem,
):
    n = wg_ref.shape[1] // CHUNKS
    blocks, rows, shard = X_WAYS * Z_WAYS, rows_ref.shape[2], wg_ref.shape[0]
    low, high = pl.ds(0, rows // 2), pl.ds(rows // 2, rows // 2)
    here, up, down, far = me.x, me.along_x(1), me.along_x(3), me.along_x(2)
    f32 = jnp.float32

    for i in range(blocks):
        at = pl.ds(i * rows, rows)
        for which in range(CORES):
            both = rows_ref[i, me.c if which == 0 else 1 - me.c]
            xp[which, at, :] = both[:, :shard]
            gp[which, at, :] = both[:, shard:]

    def copy(j, lane, src, dst, peer):
        return remote(src, dst, send_sem.at[j, lane], recv_sem.at[j, lane], peer)

    def add(ref, more):
        ref[...] = (ref[...].astype(f32) + more.astype(f32)).astype(jnp.bfloat16)

    def products(j, which, dst):
        cols = pl.ds(j * n, n)
        parts = (
            jnp.dot(xp[which], wg_ref[:, cols], preferred_element_type=f32),
            jnp.dot(xp[which], wu_ref[:, cols], preferred_element_type=f32),
            jnp.dot(gp[which], wd_ref[:, cols], preferred_element_type=f32),
        )
        for k, part in enumerate(parts):
            dst[j, :, :, :, k * n : (k + 1) * n] = part.astype(jnp.bfloat16).reshape(
                Z_WAYS, X_WAYS, rows, n
            )

    def to_partner(j):
        return copy(j, 0, away.at[j], arrived.at[j], me.partner())

    def opposite(j):
        if SUM_ORDER[j] == "x":
            return copy(j, 1, held.at[j, 1 - me.zh, here], second.at[j, 2], me.opposite())
        return copy(j, 1, held.at[j, 1 - me.zh], first.at[j], me.opposite())

    def ring_first(j, lanes=(0, 1, 2, 3)):
        mine = held.at[j, me.zh]
        if SUM_ORDER[j] == "x":
            table = (
                (held.at[j, 0, far], first.at[j, 0]),
                (held.at[j, 1, far], first.at[j, 1]),
                (held.at[j, 1, up], first.at[j, 2]),
                (held.at[j, 0, down], first.at[j, 3]),
            )
        else:
            table = (
                (mine.at[far, low], second.at[j, 2, low]),
                (mine.at[far, high], second.at[j, 2, high]),
                (mine.at[up, high], second.at[j, 0, high]),
                (mine.at[down, low], second.at[j, 1, low]),
            )
        return [copy(j, 2 + i, *table[i], me.ring(1 + 2 * (i % 2))) for i in lanes]

    def ring_second(j):
        if SUM_ORDER[j] == "x":
            return [
                copy(j, 6, held.at[j, 0, up], second.at[j, 0], me.ring(1)),
                copy(j, 7, held.at[j, 1, down], second.at[j, 1], me.ring(3)),
            ]
        mine = held.at[j, me.zh]
        return [
            copy(j, 6, mine.at[up, low], second.at[j, 0, low], me.ring(1)),
            copy(j, 7, mine.at[down, high], second.at[j, 1, high], me.ring(3)),
        ]

    def arrive(copies):
        for one in copies:
            one.wait_recv()

    def start(copies):
        for one in copies:
            one.start()

    def make(j):
        products(j, 1, away)
        to_partner(j).start()
        products(j, 0, held)

    def cores(j):
        arrive([to_partner(j)])
        for z in range(Z_WAYS):
            add(held.at[j, z], arrived[j, z])
        start(ring_first(j) if SUM_ORDER[j] == "x" else [opposite(j)])

    def pass_on(j):
        copies = ring_second(j)
        if SUM_ORDER[j] == "x":
            arrive(ring_first(j, (0,)))
            add(held.at[j, 0, up], first[j, 0])
            copies[0].start()
            arrive(ring_first(j, (1,)))
            add(held.at[j, 1, down], first[j, 1])
            copies[1].start()
        else:
            arrive(ring_first(j, (0,)))
            add(held.at[j, me.zh, up, low], second[j, 2, low])
            copies[0].start()
            arrive(ring_first(j, (1,)))
            add(held.at[j, me.zh, down, high], second[j, 2, high])
            copies[1].start()

    def gather(j):
        if SUM_ORDER[j] == "x":
            arrive(ring_first(j, (2, 3)) + ring_second(j))
            for z, (one, two) in enumerate(((second.at[j, 0], first.at[j, 3]), (second.at[j, 1], first.at[j, 2]))):
                add(held.at[j, z, here], one[...].astype(f32) + two[...].astype(f32))
            start([opposite(j)])
        else:
            arrive([opposite(j)])
            for x in (me.along_x(2), me.along_x(1), me.along_x(3), me.x):
                add(held.at[j, me.zh, x], first[j, x])
            start(ring_first(j))

    def finish(j):
        total = held[j, me.zh, here].astype(f32)
        if SUM_ORDER[j] == "x":
            arrive([opposite(j)])
            total += second[j, 2].astype(f32)
        else:
            arrive(ring_first(j, (2, 3)) + ring_second(j))
            total += second[j, 0].astype(f32) + second[j, 1].astype(f32)
        weight = pw_ref[...]
        gate, upper, back = total[:, :n], total[:, n : 2 * n], total[:, 2 * n :] * weight
        s = 1.0 / (1.0 + jnp.exp(-gate))
        out_ref[j, :, :n] = (back * upper * s * (1.0 + gate * (1.0 - s))).astype(jnp.bfloat16)
        out_ref[j, :, n:] = (back * gate * s).astype(jnp.bfloat16)
        at = (j % 2) * n
        out_ref[CHUNKS + j // 2, :, at : at + n] = (weight * gate * s * upper).astype(jnp.bfloat16)

    def middle(j, step):
        order = (pass_on, gather) if SUM_ORDER[j] == "x" else (gather, pass_on)
        order[step](j)

    def sent(j):
        for one in [to_partner(j), opposite(j)] + ring_first(j) + ring_second(j):
            one.wait_send()

    return (make, cores, lambda j: middle(j, 0), lambda j: middle(j, 1), finish), sent


def vmem(count):
    return [pl.BlockSpec(memory_space=pltpu.VMEM)] * count


Y_WAYS, PAIR = 4, 2


class Wide(Place):
    def __init__(self):
        super().__init__()
        self.d = (self.zh * X_WAYS + self.x) * CORES + self.c
        self.y, self.zl = self.expert % Y_WAYS, self.expert // Y_WAYS

    def along_y(self, k):
        return (self.y + k) % Y_WAYS

    def column(self, k):
        return (self.zl * Y_WAYS + self.along_y(k), self.d)

    def holder(self, pair, y_from, core):
        return (pair * Y_WAYS + self.y, (self.zl * X_WAYS + y_from) * CORES + core)

    def source(self, d):
        return (self.zh * Y_WAYS + self.y, d)

    def unless_self(self, peer, act):
        @pl.when((peer[0] != self.expert) | (peer[1] != self.d))
        def _():
            act()

    def greet(self, senders, others):
        barrier = pltpu.get_barrier_semaphore()
        peers = [self.column(k) for k in range(1, Y_WAYS)] + others
        for peer in peers:
            pl.semaphore_signal(barrier, inc=1, device_id=peer, device_id_type=MESH)
        for peer in senders:
            self.unless_self(
                peer,
                lambda peer=peer: pl.semaphore_signal(
                    barrier, inc=1, device_id=peer, device_id_type=MESH
                ),
            )
        pl.semaphore_wait(barrier, len(peers) + len(senders) - jnp.where(self.zl == self.zh, 1, 0))

    def holders(self):
        return [
            self.holder(p, y, core) for p in range(PAIR) for y in range(Y_WAYS) for core in range(CORES)
        ]

    def sources(self):
        return [self.source(d) for d in range(Z_WAYS * X_WAYS * CORES)]


def dispatch_kernel(
    pick_ref, x_ref, g_ref, out_ref, tok, away, mid, send1, recv1, send2, recv2
):
    me = Wide()
    shard = x_ref.shape[1] // CORES
    for h in range(CORES):
        cols = slice(h * shard, (h + 1) * shard)
        tok[h] = jnp.concatenate([x_ref[:, cols], g_ref[:, cols]], axis=1)
    me.greet(me.sources(), [])
    pieces = [(q, h) for h in range(CORES) for q in range(PAIR)]

    def pair(q):
        return (1 - me.zh + q) % PAIR

    def picked(q, h, y):
        rows = jnp.dot(pick_ref[pair(q) * Y_WAYS + y], tok[h], preferred_element_type=jnp.float32)
        return rows.astype(jnp.bfloat16)

    def to_row(q, h, k):
        return remote(
            away.at[h, me.along_y(k), pair(q)], mid.at[h, me.y, pair(q)],
            send1.at[q, h, k - 1], recv1.at[q, h, me.y], me.column(k),
        )

    def to_holder(q, h, k):
        y = me.along_y(k)
        return remote(
            mid.at[h, y, pair(q)], out_ref.at[me.d // CORES, me.c],
            send2.at[q, h, k], recv2.at[me.d], me.holder(pair(q), y, h),
        )

    for q, h in pieces:
        for k in (2, 1, 3):
            y = me.along_y(k)
            away[h, y, pair(q)] = picked(q, h, y)
            to_row(q, h, k).start()
        mid[h, me.y, pair(q)] = picked(q, h, me.y)

    for q, h in pieces:
        for k in (0, 1, 3, 2):
            y = me.along_y(k)
            if k:
                remote(
                    away.at[h, y, pair(q)], mid.at[h, y, pair(q)],
                    send1.at[q, h, 0], recv1.at[q, h, y], me.column(k),
                ).wait_recv()
            peer = me.holder(pair(q), y, h)
            me.unless_self(peer, lambda q=q, h=h, k=k: to_holder(q, h, k).start())

            @pl.when((peer[0] == me.expert) & (peer[1] == me.d))
            def _():
                out_ref[me.d // CORES, me.c] = mid[h, y, pair(q)]

    def from_source(d):
        remote(
            mid.at[0, 0, 0], out_ref.at[d // CORES, d % CORES], send2.at[0, 0, 0], recv2.at[d], me.source(d)
        ).wait_recv()

    for d in range(Z_WAYS * X_WAYS * CORES):
        me.unless_self(me.source(d), lambda d=d: from_source(d))
    for q, h in pieces:
        for k in range(1, Y_WAYS):
            to_row(q, h, k).wait_send()
        for k in range(Y_WAYS):
            me.unless_self(
                me.holder(pair(q), me.along_y(k), h), lambda q=q, h=h, k=k: to_holder(q, h, k).wait_send()
            )


def expert_kernel(
    inv_root, rows_ref, wg_ref, wu_ref, wd_ref, pw_ref, low_ref, high_ref, gg_ref, gu_ref, gd_ref, out_ref,
    act_ref, xp, gp, away, arrived, held, first, second, sum_send, sum_recv, xt, gt, whole, total, dx, mid, back, send_sem, recv_sem, send1, recv1, send2, recv2,
):
    me = Wide()
    me.greet(me.holders(), [me.partner(), me.opposite(), me.ring(1), me.ring(3)])
    sums, sums_sent = sum_stages(
        me, rows_ref, wg_ref, wu_ref, wd_ref, pw_ref, act_ref,
        xp, gp, away, arrived, held, first, second, sum_send, sum_recv,
    )
    n = wg_ref.shape[1] // CHUNKS
    blocks, rows, shard = X_WAYS * Z_WAYS, rows_ref.shape[2], wg_ref.shape[0]
    slots = CORES * blocks * rows
    low, high = pl.ds(0, rows // 2), pl.ds(rows // 2, rows // 2)
    here, up, down = me.x, me.along_x(1), me.along_x(3)
    f32 = jnp.float32
    spread_chunks = len(SPREAD_ORDER)

    def copy(j, lane, src, dst, peer):
        return remote(src, dst, send_sem.at[j, lane], recv_sem.at[j, lane], peer)

    def part(j, x, half=None):
        if half is None:
            return whole.at[j, 0, me.zh, x] if SPREAD_ORDER[j] == "x" else whole.at[j, 0, :, x]
        return whole.at[j, 0, me.zh, x, half] if SPREAD_ORDER[j] == "x" else whole.at[j, 0, :, x, half]

    def neighbours(j):
        src = act_ref.at[j] if SPREAD_ORDER[j] == "x" else part(j, here)
        return [copy(j, 2, src, part(j, here), me.ring(1)), copy(j, 3, src, part(j, here), me.ring(3))]

    def passed(j):
        return [
            copy(j, 4, part(j, down, low), part(j, down, low), me.ring(1)),
            copy(j, 5, part(j, up, high), part(j, up, high), me.ring(3)),
        ]

    def opposite(j):
        if SPREAD_ORDER[j] == "x":
            return copy(j, 1, whole.at[j, 0, me.zh], whole.at[j, 0, me.zh], me.opposite())
        return copy(j, 1, act_ref.at[j], whole.at[j, 0, me.zh, here], me.opposite())

    def to_partner(j):
        return copy(j, 0, whole.at[j, 0], whole.at[j, 1], me.partner())

    def begin(j):
        if SPREAD_ORDER[j] == "x":
            for one in neighbours(j):
                one.start()
        else:
            opposite(j).start()
        whole[j, 0, me.zh, here] = act_ref[j]

    def relay(j):
        for one, on in zip(neighbours(j), passed(j)):
            one.wait_recv()
            on.start()

    def middle(j, step):
        if SPREAD_ORDER[j] == "x":
            if step == 0:
                relay(j)
            else:
                for one in passed(j):
                    one.wait_recv()
                opposite(j).start()
        elif step == 0:
            opposite(j).wait_recv()
            for one in neighbours(j):
                one.start()
        else:
            relay(j)

    def cores(j):
        if SPREAD_ORDER[j] == "x":
            opposite(j).wait_recv()
        else:
            for one in passed(j):
                one.wait_recv()
        to_partner(j).start()

    def grad(turned, j, cols):
        both = whole[j, :, :, :, :, cols].reshape(slots, -1)
        return (jnp.dot(turned[...], both, preferred_element_type=f32) * inv_root).astype(jnp.bfloat16)

    def inputs(j):
        to_partner(j).wait_recv()
        cols = pl.ds(j * n, n)
        d_gate = whole[j, :, :, :, :, :n].reshape(slots, n)
        d_up = whole[j, :, :, :, :, n:].reshape(slots, n)
        more = lax.dot_general(d_gate, wg_ref[:, cols], LAST, preferred_element_type=f32)
        more += lax.dot_general(d_up, wu_ref[:, cols], LAST, preferred_element_type=f32)
        total[...] = more if j == 0 else total[...] + more

    def weights(j):
        if j < CHUNKS:
            cols = pl.ds(j * n, n)
            gg_ref[:, cols] = grad(xt, j, slice(0, n))
            gu_ref[:, cols] = grad(xt, j, slice(n, 2 * n))
        else:
            to_partner(j).wait_recv()
            gd_ref[:, pl.ds((j - CHUNKS) * 2 * n, 2 * n)] = grad(gt, j, slice(0, 2 * n))

    def to_source(d):
        return remote(
            dx.at[d // CORES, d % CORES], mid.at[me.x, me.zl, me.c], send1.at[d],
            recv1.at[me.x, me.zl, me.c], me.source(d),
        )

    def to_column(k):
        y = me.along_y(k)
        return remote(mid.at[y], back.at[me.y], send2.at[k - 1], recv2.at[me.y], me.column(k))

    def home_first():
        for i in range(blocks):
            for which in range(CORES):
                at = (which * blocks + i) * rows
                one = total[at : at + rows // 2, :].astype(jnp.bfloat16)
                two = total[at + rows // 2 : at + rows, :].astype(jnp.bfloat16)
                dx[i, me.c if which == 0 else 1 - me.c] = jnp.concatenate([one, two], axis=1)
        for k in range(Z_WAYS * X_WAYS * CORES):
            d = (me.d + k + 4) % (Z_WAYS * X_WAYS * CORES)
            me.unless_self(me.source(d), lambda d=d: to_source(d).start())

        @pl.when(me.zl == me.zh)
        def _():
            mid[me.x, me.zl, me.c] = dx[me.d // CORES, me.c]

    def from_holder(p, y, core):
        peer = me.holder(p, y, core)

        def wait():
            remote(
                dx.at[0, 0], mid.at[y, p, core], send1.at[0], recv1.at[y, p, core], peer
            ).wait_recv()

        me.unless_self(peer, wait)

    def home_second():
        for k in (2, 1, 3, 0):
            y = me.along_y(k)
            for p in range(PAIR):
                for core in range(CORES):
                    from_holder(p, y, core)
            if k:
                to_column(k).start()
        back[me.y] = mid[me.y]

    def home():
        for k in range(1, Y_WAYS):
            y = me.along_y(k)
            remote(mid.at[0], back.at[y], send2.at[0], recv2.at[y], me.column(k)).wait_recv()
        parts = []
        for h in range(CORES):
            blocks_of = back[:, :, h].reshape(low_ref.shape[1], CORES * shard)
            one = jnp.dot(low_ref[...], blocks_of, preferred_element_type=f32)
            two = jnp.dot(high_ref[...], blocks_of, preferred_element_type=f32)
            parts.append(one[:, :shard] + two[:, shard:])
        out_ref[...] = jnp.concatenate(parts, axis=1).astype(jnp.bfloat16)

    def turn(turned, lo):
        for i in range(blocks):
            for which in range(CORES):
                at = pl.ds((which * blocks + i) * rows, rows)
                c = me.c if which == 0 else 1 - me.c
                total[at, :] = rows_ref[i, c][:, lo : lo + shard].astype(f32)
        turned[...] = total[...].T.astype(jnp.bfloat16)

    late = range(CHUNKS, spread_chunks)
    stages = (lambda j: middle(j, 0), lambda j: middle(j, 1), cores, inputs)
    line = sums + (begin,) + stages
    lags = SUM_LAGS + tuple(SUM_LAGS[-1] + lag for lag in (0,) + SPREAD_LAGS)
    for t in range(CHUNKS + lags[-1]):
        for stage, lag in zip(line, lags):
            if 0 <= t - lag < CHUNKS:
                stage(t - lag)
        if t - SUM_LAGS[-1] - LATE_LAG in range(spread_chunks - CHUNKS):
            begin(CHUNKS + t - SUM_LAGS[-1] - LATE_LAG)
    home_first()
    for j in late:
        stages[0](j)
    turn(xt, 0)
    for j in late:
        weights(2 * (j - CHUNKS))
        stages[1](j)
    turn(gt, shard)
    home_second()
    for j in late:
        cores(j)
        weights(2 * (j - CHUNKS) + 1)
    for j in late:
        weights(j)
    home()
    for j in range(CHUNKS):
        sums_sent(j)
    for j in range(spread_chunks):
        for one in [to_partner(j), opposite(j)] + neighbours(j) + passed(j):
            one.wait_send()
    for d in range(Z_WAYS * X_WAYS * CORES):
        me.unless_self(me.source(d), lambda d=d: to_source(d).wait_send())
    for k in range(1, Y_WAYS):
        to_column(k).wait_send()


def dispatched(pick, x, g):
    (_, rows, _), (tokens, width) = pick.shape, x.shape
    bf16 = jnp.bfloat16
    groups = X_WAYS * Z_WAYS
    dma = pltpu.SemaphoreType.DMA
    return pl.pallas_call(
        dispatch_kernel,
        out_shape=jax.ShapeDtypeStruct((groups, CORES, rows, width), bf16),
        in_specs=vmem(3),
        out_specs=vmem(1)[0],
        scratch_shapes=[
            pltpu.VMEM((CORES, tokens, width), bf16),
            pltpu.VMEM((CORES, Y_WAYS, PAIR, rows, width), bf16),
            pltpu.VMEM((CORES, Y_WAYS, PAIR, rows, width), bf16),
            dma((PAIR, CORES, Y_WAYS - 1)),
            dma((PAIR, CORES, Y_WAYS)),
            dma((PAIR, CORES, Y_WAYS)),
            dma((groups * CORES,)),
        ],
        compiler_params=pltpu.CompilerParams(
            collective_id=2, has_side_effects=True, vmem_limit_bytes=20 << 20
        ),
    )(pick, x, g)


def expert_rows(inv_root, packed, w_gate, w_up, w_down, weight, low, high):
    (blocks, cores, rows, width), (shard, hidden) = packed.shape, w_gate.shape
    cols, sum_cols = 2 * hidden // CHUNKS, 3 * hidden // CHUNKS
    slots = cores * blocks * rows
    count = len(SPREAD_ORDER)
    bf16, dma = jnp.bfloat16, pltpu.SemaphoreType.DMA
    return pl.pallas_call(
        functools.partial(expert_kernel, inv_root),
        out_shape=(
            jax.ShapeDtypeStruct((shard, hidden), bf16),
            jax.ShapeDtypeStruct((shard, hidden), bf16),
            jax.ShapeDtypeStruct((shard, hidden), bf16),
            jax.ShapeDtypeStruct((low.shape[0], width), bf16),
        ),
        in_specs=vmem(7),
        out_specs=vmem(4),
        scratch_shapes=[
            pltpu.VMEM((count, rows, cols), bf16),
            pltpu.VMEM((cores, blocks * rows, shard), bf16),
            pltpu.VMEM((cores, blocks * rows, shard), bf16),
            pltpu.VMEM((CHUNKS, Z_WAYS, X_WAYS, rows, sum_cols), bf16),
            pltpu.VMEM((CHUNKS, Z_WAYS, X_WAYS, rows, sum_cols), bf16),
            pltpu.VMEM((CHUNKS, Z_WAYS, X_WAYS, rows, sum_cols), bf16),
            pltpu.VMEM((CHUNKS, X_WAYS, rows, sum_cols), bf16),
            pltpu.VMEM((CHUNKS, X_WAYS - 1, rows, sum_cols), bf16),
            dma((CHUNKS, 8)),
            dma((CHUNKS, 8)),
            pltpu.VMEM((shard, slots), bf16),
            pltpu.VMEM((shard, slots), bf16),
            pltpu.VMEM((count, cores, Z_WAYS, X_WAYS, rows, cols), bf16),
            pltpu.VMEM((slots, shard), jnp.float32),
            pltpu.VMEM((blocks, cores, rows // 2, width), bf16),
            pltpu.VMEM((Y_WAYS, PAIR, cores, rows // 2, width), bf16),
            pltpu.VMEM((Y_WAYS, PAIR, cores, rows // 2, width), bf16),
            dma((count, 6)),
            dma((count, 6)),
            dma((blocks * cores,)),
            dma((Y_WAYS, PAIR, cores)),
            dma((Y_WAYS - 1,)),
            dma((Y_WAYS,)),
        ],
        compiler_params=pltpu.CompilerParams(
            collective_id=0, has_side_effects=True, vmem_limit_bytes=59 << 20
        ),
    )(packed, w_gate, w_up, w_down, weight, low, high)


def body(tokens, grad_out, expert_ids, route_weights, w_gate, w_up, w_down):
    experts = lax.axis_size("expert")
    groups = lax.axis_size("dp")
    tok_rows = tokens.shape[0]
    capacity = tok_rows // 2
    expert_index = lax.axis_index("expert")
    inv_root = 1.0 / math.sqrt(tok_rows * groups)
    gate_shard, up_shard, down_shard = w_gate[0], w_up[0], w_down[0].T

    names = jnp.arange(experts, dtype=jnp.int32)[:, None]
    hit0 = expert_ids[:, 0][None, :] == names
    hit1 = expert_ids[:, 1][None, :] == names
    hit = (hit0 | hit1).astype(jnp.bfloat16)
    index = jnp.arange(tok_rows, dtype=jnp.int32)
    before = (index[:, None] < index[None, :]).astype(jnp.bfloat16)
    rank = jnp.dot(hit, before, preferred_element_type=jnp.float32)
    rank = jnp.where(hit > 0, rank, -1.0).astype(jnp.int32)
    chosen = rank[:, None, :] == jnp.arange(capacity, dtype=jnp.int32)[None, :, None]
    pick = chosen.astype(jnp.bfloat16)

    def place(first):
        by_row = rank.reshape(PAIR, Y_WAYS, tok_rows).transpose(2, 1, 0).reshape(tok_rows, experts)
        part = by_row[:, :, None] == jnp.arange(first, first + capacity // 2, dtype=jnp.int32)
        return part.astype(jnp.bfloat16).reshape(tok_rows, experts * capacity // 2)

    weight_of = jnp.where(hit0, route_weights[:, 0][None, :], 0.0) + jnp.where(
        hit1, route_weights[:, 1][None, :], 0.0
    )
    own_rank = lax.dynamic_slice_in_dim(rank, expert_index, 1)
    own_weight_of = lax.dynamic_slice_in_dim(weight_of, expert_index, 1)
    own_weight = jnp.sum(
        jnp.where(
            own_rank == jnp.arange(capacity, dtype=jnp.int32)[:, None], own_weight_of, 0.0
        ),
        axis=1,
    )

    packed = dispatched(pick, tokens, grad_out)
    grad_g, grad_u, grad_d, grad_tokens = expert_rows(
        inv_root, packed, gate_shard, up_shard, down_shard, own_weight[:, None],
        place(0), place(capacity // 2),
    )
    return (grad_tokens, grad_g[None], grad_u[None], grad_d.T[None])


def solution(mesh):
    in_specs = (
        P("dp", "expert"),
        P("dp", "expert"),
        P("dp", None),
        P("dp", None),
        P("expert", "dp", None),
        P("expert", "dp", None),
        P("expert", None, "dp"),
    )
    out_specs = (
        P("dp", "expert"),
        P("expert", "dp", None),
        P("expert", "dp", None),
        P("expert", None, "dp"),
    )
    return jax.shard_map(body, mesh=mesh, in_specs=in_specs, out_specs=out_specs, check_vma=False)
```

```python
import functools
import math

import jax
import jax.numpy as jnp
from jax import lax
from jax.experimental import pallas as pl
from jax.experimental.pallas import tpu as pltpu
from jax.sharding import PartitionSpec as P

MESH = pl.DeviceIdType.MESH
CHUNKS = 8
X_WAYS, Z_WAYS, CORES = 4, 2, 2
LAST = (((1,), (1,)), ((), ()))
SUM_ORDER = "xzxzxxzx"
SPREAD_ORDER = "xzxzzxzzzzzx"
SUM_LAGS = (0, 1, 4, 6, 8)
SPREAD_LAGS = (2, 4, 6, 7)
LATE_LAG = 8


class Place:
    def __init__(self):
        self.expert = lax.axis_index("expert")
        d = lax.axis_index("dp")
        self.c = d % CORES
        self.x = (d // CORES) % X_WAYS
        self.zh = d // (CORES * X_WAYS)

    def at(self, zh, x, c):
        return (self.expert, (zh * X_WAYS + x) * CORES + c)

    def partner(self):
        return self.at(self.zh, self.x, 1 - self.c)

    def opposite(self):
        return self.at(1 - self.zh, self.x, self.c)

    def along_x(self, k):
        return (self.x + k) % X_WAYS

    def ring(self, k):
        return self.at(self.zh, self.along_x(k), self.c)

    def greet(self):
        barrier = pltpu.get_barrier_semaphore()
        peers = [self.partner(), self.opposite(), self.ring(1), self.ring(3)]
        for peer in peers:
            pl.semaphore_signal(barrier, inc=1, device_id=peer, device_id_type=MESH)
        pl.semaphore_wait(barrier, len(peers))


def remote(src, dst, send_sem, recv_sem, peer):
    return pltpu.make_async_remote_copy(
        src_ref=src, dst_ref=dst, send_sem=send_sem, recv_sem=recv_sem,
        device_id=peer, device_id_type=MESH,
    )


def sum_stages(
    me, rows_ref, wg_ref, wu_ref, wd_ref, pw_ref, out_ref,
    xp, gp, away, arrived, held, first, second, send_sem, recv_sem,
):
    n = wg_ref.shape[1] // CHUNKS
    blocks, rows, shard = X_WAYS * Z_WAYS, rows_ref.shape[2], wg_ref.shape[0]
    low, high = pl.ds(0, rows // 2), pl.ds(rows // 2, rows // 2)
    here, up, down, far = me.x, me.along_x(1), me.along_x(3), me.along_x(2)
    f32 = jnp.float32

    for i in range(blocks):
        at = pl.ds(i * rows, rows)
        for which in range(CORES):
            both = rows_ref[i, me.c if which == 0 else 1 - me.c]
            xp[which, at, :] = both[:, :shard]
            gp[which, at, :] = both[:, shard:]

    def copy(j, lane, src, dst, peer):
        return remote(src, dst, send_sem.at[j, lane], recv_sem.at[j, lane], peer)

    def add(ref, more):
        ref[...] = (ref[...].astype(f32) + more.astype(f32)).astype(jnp.bfloat16)

    def products(j, which, dst):
        cols = pl.ds(j * n, n)
        parts = (
            jnp.dot(xp[which], wg_ref[:, cols], preferred_element_type=f32),
            jnp.dot(xp[which], wu_ref[:, cols], preferred_element_type=f32),
            jnp.dot(gp[which], wd_ref[:, cols], preferred_element_type=f32),
        )
        for k, part in enumerate(parts):
            dst[j, :, :, :, k * n : (k + 1) * n] = part.astype(jnp.bfloat16).reshape(
                Z_WAYS, X_WAYS, rows, n
            )

    def to_partner(j):
        return copy(j, 0, away.at[j], arrived.at[j], me.partner())

    def opposite(j):
        if SUM_ORDER[j] == "x":
            return copy(j, 1, held.at[j, 1 - me.zh, here], second.at[j, 2], me.opposite())
        return copy(j, 1, held.at[j, 1 - me.zh], first.at[j], me.opposite())

    def ring_first(j, lanes=(0, 1, 2, 3)):
        mine = held.at[j, me.zh]
        if SUM_ORDER[j] == "x":
            table = (
                (held.at[j, 0, far], first.at[j, 0]),
                (held.at[j, 1, far], first.at[j, 1]),
                (held.at[j, 1, up], first.at[j, 2]),
                (held.at[j, 0, down], first.at[j, 3]),
            )
        else:
            table = (
                (mine.at[far, low], second.at[j, 2, low]),
                (mine.at[far, high], second.at[j, 2, high]),
                (mine.at[up, high], second.at[j, 0, high]),
                (mine.at[down, low], second.at[j, 1, low]),
            )
        return [copy(j, 2 + i, *table[i], me.ring(1 + 2 * (i % 2))) for i in lanes]

    def ring_second(j):
        if SUM_ORDER[j] == "x":
            return [
                copy(j, 6, held.at[j, 0, up], second.at[j, 0], me.ring(1)),
                copy(j, 7, held.at[j, 1, down], second.at[j, 1], me.ring(3)),
            ]
        mine = held.at[j, me.zh]
        return [
            copy(j, 6, mine.at[up, low], second.at[j, 0, low], me.ring(1)),
            copy(j, 7, mine.at[down, high], second.at[j, 1, high], me.ring(3)),
        ]

    def arrive(copies):
        for one in copies:
            one.wait_recv()

    def start(copies):
        for one in copies:
            one.start()

    def make(j):
        products(j, 1, away)
        to_partner(j).start()
        products(j, 0, held)

    def cores(j):
        arrive([to_partner(j)])
        for z in range(Z_WAYS):
            add(held.at[j, z], arrived[j, z])
        start(ring_first(j) if SUM_ORDER[j] == "x" else [opposite(j)])

    def pass_on(j):
        copies = ring_second(j)
        if SUM_ORDER[j] == "x":
            arrive(ring_first(j, (0,)))
            add(held.at[j, 0, up], first[j, 0])
            copies[0].start()
            arrive(ring_first(j, (1,)))
            add(held.at[j, 1, down], first[j, 1])
            copies[1].start()
        else:
            arrive(ring_first(j, (0,)))
            add(held.at[j, me.zh, up, low], second[j, 2, low])
            copies[0].start()
            arrive(ring_first(j, (1,)))
            add(held.at[j, me.zh, down, high], second[j, 2, high])
            copies[1].start()

    def gather(j):
        if SUM_ORDER[j] == "x":
            arrive(ring_first(j, (2, 3)) + ring_second(j))
            for z, (one, two) in enumerate(((second.at[j, 0], first.at[j, 3]), (second.at[j, 1], first.at[j, 2]))):
                add(held.at[j, z, here], one[...].astype(f32) + two[...].astype(f32))
            start([opposite(j)])
        else:
            arrive([opposite(j)])
            for x in (me.along_x(2), me.along_x(1), me.along_x(3), me.x):
                add(held.at[j, me.zh, x], first[j, x])
            start(ring_first(j))

    def finish(j):
        total = held[j, me.zh, here].astype(f32)
        if SUM_ORDER[j] == "x":
            arrive([opposite(j)])
            total += second[j, 2].astype(f32)
        else:
            arrive(ring_first(j, (2, 3)) + ring_second(j))
            total += second[j, 0].astype(f32) + second[j, 1].astype(f32)
        weight = pw_ref[...]
        gate, upper, back = total[:, :n], total[:, n : 2 * n], total[:, 2 * n :] * weight
        s = 1.0 / (1.0 + jnp.exp(-gate))
        out_ref[j, :, :n] = (back * upper * s * (1.0 + gate * (1.0 - s))).astype(jnp.bfloat16)
        out_ref[j, :, n:] = (back * gate * s).astype(jnp.bfloat16)
        at = (j % 2) * n
        out_ref[CHUNKS + j // 2, :, at : at + n] = (weight * gate * s * upper).astype(jnp.bfloat16)

    def middle(j, step):
        order = (pass_on, gather) if SUM_ORDER[j] == "x" else (gather, pass_on)
        order[step](j)

    def sent(j):
        for one in [to_partner(j), opposite(j)] + ring_first(j) + ring_second(j):
            one.wait_send()

    return (make, cores, lambda j: middle(j, 0), lambda j: middle(j, 1), finish), sent


def vmem(count):
    return [pl.BlockSpec(memory_space=pltpu.VMEM)] * count


Y_WAYS, PAIR = 4, 2


class Wide(Place):
    def __init__(self):
        super().__init__()
        self.d = (self.zh * X_WAYS + self.x) * CORES + self.c
        self.y, self.zl = self.expert % Y_WAYS, self.expert // Y_WAYS

    def along_y(self, k):
        return (self.y + k) % Y_WAYS

    def column(self, k):
        return (self.zl * Y_WAYS + self.along_y(k), self.d)

    def holder(self, pair, y_from, core):
        return (pair * Y_WAYS + self.y, (self.zl * X_WAYS + y_from) * CORES + core)

    def source(self, d):
        return (self.zh * Y_WAYS + self.y, d)

    def unless_self(self, peer, act):
        @pl.when((peer[0] != self.expert) | (peer[1] != self.d))
        def _():
            act()

    def greet(self, senders, others):
        barrier = pltpu.get_barrier_semaphore()
        peers = [self.column(k) for k in range(1, Y_WAYS)] + others
        for peer in peers:
            pl.semaphore_signal(barrier, inc=1, device_id=peer, device_id_type=MESH)
        for peer in senders:
            self.unless_self(
                peer,
                lambda peer=peer: pl.semaphore_signal(
                    barrier, inc=1, device_id=peer, device_id_type=MESH
                ),
            )
        pl.semaphore_wait(barrier, len(peers) + len(senders) - jnp.where(self.zl == self.zh, 1, 0))

    def holders(self):
        return [
            self.holder(p, y, core) for p in range(PAIR) for y in range(Y_WAYS) for core in range(CORES)
        ]

    def sources(self):
        return [self.source(d) for d in range(Z_WAYS * X_WAYS * CORES)]


def dispatch_kernel(
    pick_ref, x_ref, g_ref, out_ref, tok, away, mid, send1, recv1, send2, recv2
):
    me = Wide()
    shard = x_ref.shape[1] // CORES
    for h in range(CORES):
        cols = slice(h * shard, (h + 1) * shard)
        tok[h] = jnp.concatenate([x_ref[:, cols], g_ref[:, cols]], axis=1)
    me.greet(me.sources(), [])
    pieces = [(q, h) for h in range(CORES) for q in range(PAIR)]

    def pair(q):
        return (1 - me.zh + q) % PAIR

    def picked(q, h, y):
        rows = jnp.dot(pick_ref[pair(q) * Y_WAYS + y], tok[h], preferred_element_type=jnp.float32)
        return rows.astype(jnp.bfloat16)

    def to_row(q, h, k):
        return remote(
            away.at[h, me.along_y(k), pair(q)], mid.at[h, me.y, pair(q)],
            send1.at[q, h, k - 1], recv1.at[q, h, me.y], me.column(k),
        )

    def to_holder(q, h, k):
        y = me.along_y(k)
        return remote(
            mid.at[h, y, pair(q)], out_ref.at[me.d // CORES, me.c],
            send2.at[q, h, k], recv2.at[me.d], me.holder(pair(q), y, h),
        )

    for q, h in pieces:
        for k in (2, 1, 3):
            y = me.along_y(k)
            away[h, y, pair(q)] = picked(q, h, y)
            to_row(q, h, k).start()
        mid[h, me.y, pair(q)] = picked(q, h, me.y)

    for q, h in pieces:
        for k in (0, 1, 3, 2):
            y = me.along_y(k)
            if k:
                remote(
                    away.at[h, y, pair(q)], mid.at[h, y, pair(q)],
                    send1.at[q, h, 0], recv1.at[q, h, y], me.column(k),
                ).wait_recv()
            peer = me.holder(pair(q), y, h)
            me.unless_self(peer, lambda q=q, h=h, k=k: to_holder(q, h, k).start())

            @pl.when((peer[0] == me.expert) & (peer[1] == me.d))
            def _():
                out_ref[me.d // CORES, me.c] = mid[h, y, pair(q)]

    def from_source(d):
        remote(
            mid.at[0, 0, 0], out_ref.at[d // CORES, d % CORES], send2.at[0, 0, 0], recv2.at[d], me.source(d)
        ).wait_recv()

    for d in range(Z_WAYS * X_WAYS * CORES):
        me.unless_self(me.source(d), lambda d=d: from_source(d))
    for q, h in pieces:
        for k in range(1, Y_WAYS):
            to_row(q, h, k).wait_send()
        for k in range(Y_WAYS):
            me.unless_self(
                me.holder(pair(q), me.along_y(k), h), lambda q=q, h=h, k=k: to_holder(q, h, k).wait_send()
            )


def expert_kernel(
    inv_root, rows_ref, wg_ref, wu_ref, wd_ref, pw_ref, low_ref, high_ref, gg_ref, gu_ref, gd_ref, out_ref,
    act_ref, xp, gp, away, arrived, held, first, second, sum_send, sum_recv, xt, gt, whole, total, dx, mid, back, send_sem, recv_sem, send1, recv1, send2, recv2,
):
    me = Wide()
    me.greet(me.holders(), [me.partner(), me.opposite(), me.ring(1), me.ring(3)])
    sums, sums_sent = sum_stages(
        me, rows_ref, wg_ref, wu_ref, wd_ref, pw_ref, act_ref,
        xp, gp, away, arrived, held, first, second, sum_send, sum_recv,
    )
    n = wg_ref.shape[1] // CHUNKS
    blocks, rows, shard = X_WAYS * Z_WAYS, rows_ref.shape[2], wg_ref.shape[0]
    slots = CORES * blocks * rows
    low, high = pl.ds(0, rows // 2), pl.ds(rows // 2, rows // 2)
    here, up, down = me.x, me.along_x(1), me.along_x(3)
    f32 = jnp.float32
    spread_chunks = len(SPREAD_ORDER)

    def copy(j, lane, src, dst, peer):
        return remote(src, dst, send_sem.at[j, lane], recv_sem.at[j, lane], peer)

    def part(j, x, half=None):
        if half is None:
            return whole.at[j, 0, me.zh, x] if SPREAD_ORDER[j] == "x" else whole.at[j, 0, :, x]
        return whole.at[j, 0, me.zh, x, half] if SPREAD_ORDER[j] == "x" else whole.at[j, 0, :, x, half]

    def neighbours(j):
        src = act_ref.at[j] if SPREAD_ORDER[j] == "x" else part(j, here)
        return [copy(j, 2, src, part(j, here), me.ring(1)), copy(j, 3, src, part(j, here), me.ring(3))]

    def passed(j):
        return [
            copy(j, 4, part(j, down, low), part(j, down, low), me.ring(1)),
            copy(j, 5, part(j, up, high), part(j, up, high), me.ring(3)),
        ]

    def opposite(j):
        if SPREAD_ORDER[j] == "x":
            return copy(j, 1, whole.at[j, 0, me.zh], whole.at[j, 0, me.zh], me.opposite())
        return copy(j, 1, act_ref.at[j], whole.at[j, 0, me.zh, here], me.opposite())

    def to_partner(j):
        return copy(j, 0, whole.at[j, 0], whole.at[j, 1], me.partner())

    def begin(j):
        if SPREAD_ORDER[j] == "x":
            for one in neighbours(j):
                one.start()
        else:
            opposite(j).start()
        whole[j, 0, me.zh, here] = act_ref[j]

    def relay(j):
        for one, on in zip(neighbours(j), passed(j)):
            one.wait_recv()
            on.start()

    def middle(j, step):
        if SPREAD_ORDER[j] == "x":
            if step == 0:
                relay(j)
            else:
                for one in passed(j):
                    one.wait_recv()
                opposite(j).start()
        elif step == 0:
            opposite(j).wait_recv()
            for one in neighbours(j):
                one.start()
        else:
            relay(j)

    def cores(j):
        if SPREAD_ORDER[j] == "x":
            opposite(j).wait_recv()
        else:
            for one in passed(j):
                one.wait_recv()
        to_partner(j).start()

    def grad(turned, j, cols):
        both = whole[j, :, :, :, :, cols].reshape(slots, -1)
        return (jnp.dot(turned[...], both, preferred_element_type=f32) * inv_root).astype(jnp.bfloat16)

    def inputs(j):
        to_partner(j).wait_recv()
        cols = pl.ds(j * n, n)
        d_gate = whole[j, :, :, :, :, :n].reshape(slots, n)
        d_up = whole[j, :, :, :, :, n:].reshape(slots, n)
        more = lax.dot_general(d_gate, wg_ref[:, cols], LAST, preferred_element_type=f32)
        more += lax.dot_general(d_up, wu_ref[:, cols], LAST, preferred_element_type=f32)
        total[...] = more if j == 0 else total[...] + more

    def weights(j):
        if j < CHUNKS:
            cols = pl.ds(j * n, n)
            gg_ref[:, cols] = grad(xt, j, slice(0, n))
            gu_ref[:, cols] = grad(xt, j, slice(n, 2 * n))
        else:
            to_partner(j).wait_recv()
            gd_ref[:, pl.ds((j - CHUNKS) * 2 * n, 2 * n)] = grad(gt, j, slice(0, 2 * n))

    def to_source(d):
        return remote(
            dx.at[d // CORES, d % CORES], mid.at[me.x, me.zl, me.c], send1.at[d],
            recv1.at[me.x, me.zl, me.c], me.source(d),
        )

    def to_column(k):
        y = me.along_y(k)
        return remote(mid.at[y], back.at[me.y], send2.at[k - 1], recv2.at[me.y], me.column(k))

    def home_first():
        for i in range(blocks):
            for which in range(CORES):
                at = (which * blocks + i) * rows
                one = total[at : at + rows // 2, :].astype(jnp.bfloat16)
                two = total[at + rows // 2 : at + rows, :].astype(jnp.bfloat16)
                dx[i, me.c if which == 0 else 1 - me.c] = jnp.concatenate([one, two], axis=1)
        for k in range(Z_WAYS * X_WAYS * CORES):
            d = (me.d + k + 4) % (Z_WAYS * X_WAYS * CORES)
            me.unless_self(me.source(d), lambda d=d: to_source(d).start())

        @pl.when(me.zl == me.zh)
        def _():
            mid[me.x, me.zl, me.c] = dx[me.d // CORES, me.c]

    def from_holder(p, y, core):
        peer = me.holder(p, y, core)

        def wait():
            remote(
                dx.at[0, 0], mid.at[y, p, core], send1.at[0], recv1.at[y, p, core], peer
            ).wait_recv()

        me.unless_self(peer, wait)

    def home_second():
        for k in (2, 1, 3, 0):
            y = me.along_y(k)
            for p in range(PAIR):
                for core in range(CORES):
                    from_holder(p, y, core)
            if k:
                to_column(k).start()
        back[me.y] = mid[me.y]

    def home():
        for k in range(1, Y_WAYS):
            y = me.along_y(k)
            remote(mid.at[0], back.at[y], send2.at[0], recv2.at[y], me.column(k)).wait_recv()
        parts = []
        for h in range(CORES):
            blocks_of = back[:, :, h].reshape(low_ref.shape[1], CORES * shard)
            one = jnp.dot(low_ref[...], blocks_of, preferred_element_type=f32)
            two = jnp.dot(high_ref[...], blocks_of, preferred_element_type=f32)
            parts.append(one[:, :shard] + two[:, shard:])
        out_ref[...] = jnp.concatenate(parts, axis=1).astype(jnp.bfloat16)

    def turn(turned, lo):
        for i in range(blocks):
            for which in range(CORES):
                at = pl.ds((which * blocks + i) * rows, rows)
                c = me.c if which == 0 else 1 - me.c
                total[at, :] = rows_ref[i, c][:, lo : lo + shard].astype(f32)
        turned[...] = total[...].T.astype(jnp.bfloat16)

    late = range(CHUNKS, spread_chunks)
    stages = (lambda j: middle(j, 0), lambda j: middle(j, 1), cores, inputs)
    line = sums + (begin,) + stages
    lags = SUM_LAGS + tuple(SUM_LAGS[-1] + lag for lag in (0,) + SPREAD_LAGS)
    for t in range(CHUNKS + lags[-1]):
        for stage, lag in zip(line, lags):
            if 0 <= t - lag < CHUNKS:
                stage(t - lag)
        if t - SUM_LAGS[-1] - LATE_LAG in range(spread_chunks - CHUNKS):
            begin(CHUNKS + t - SUM_LAGS[-1] - LATE_LAG)
    home_first()
    for j in late:
        stages[0](j)
    turn(xt, 0)
    for j in late:
        weights(2 * (j - CHUNKS))
        stages[1](j)
    home_second()
    turn(gt, shard)
    for j in late:
        cores(j)
        weights(2 * (j - CHUNKS) + 1)
    for j in late:
        weights(j)
    home()
    for j in range(CHUNKS):
        sums_sent(j)
    for j in range(spread_chunks):
        for one in [to_partner(j), opposite(j)] + neighbours(j) + passed(j):
            one.wait_send()
    for d in range(Z_WAYS * X_WAYS * CORES):
        me.unless_self(me.source(d), lambda d=d: to_source(d).wait_send())
    for k in range(1, Y_WAYS):
        to_column(k).wait_send()


def dispatched(pick, x, g):
    (_, rows, _), (tokens, width) = pick.shape, x.shape
    bf16 = jnp.bfloat16
    groups = X_WAYS * Z_WAYS
    dma = pltpu.SemaphoreType.DMA
    return pl.pallas_call(
        dispatch_kernel,
        out_shape=jax.ShapeDtypeStruct((groups, CORES, rows, width), bf16),
        in_specs=vmem(3),
        out_specs=vmem(1)[0],
        scratch_shapes=[
            pltpu.VMEM((CORES, tokens, width), bf16),
            pltpu.VMEM((CORES, Y_WAYS, PAIR, rows, width), bf16),
            pltpu.VMEM((CORES, Y_WAYS, PAIR, rows, width), bf16),
            dma((PAIR, CORES, Y_WAYS - 1)),
            dma((PAIR, CORES, Y_WAYS)),
            dma((PAIR, CORES, Y_WAYS)),
            dma((groups * CORES,)),
        ],
        compiler_params=pltpu.CompilerParams(
            collective_id=2, has_side_effects=True, vmem_limit_bytes=20 << 20
        ),
    )(pick, x, g)


def expert_rows(inv_root, packed, w_gate, w_up, w_down, weight, low, high):
    (blocks, cores, rows, width), (shard, hidden) = packed.shape, w_gate.shape
    cols, sum_cols = 2 * hidden // CHUNKS, 3 * hidden // CHUNKS
    slots = cores * blocks * rows
    count = len(SPREAD_ORDER)
    bf16, dma = jnp.bfloat16, pltpu.SemaphoreType.DMA
    return pl.pallas_call(
        functools.partial(expert_kernel, inv_root),
        out_shape=(
            jax.ShapeDtypeStruct((shard, hidden), bf16),
            jax.ShapeDtypeStruct((shard, hidden), bf16),
            jax.ShapeDtypeStruct((shard, hidden), bf16),
            jax.ShapeDtypeStruct((low.shape[0], width), bf16),
        ),
        in_specs=vmem(7),
        out_specs=vmem(4),
        scratch_shapes=[
            pltpu.VMEM((count, rows, cols), bf16),
            pltpu.VMEM((cores, blocks * rows, shard), bf16),
            pltpu.VMEM((cores, blocks * rows, shard), bf16),
            pltpu.VMEM((CHUNKS, Z_WAYS, X_WAYS, rows, sum_cols), bf16),
            pltpu.VMEM((CHUNKS, Z_WAYS, X_WAYS, rows, sum_cols), bf16),
            pltpu.VMEM((CHUNKS, Z_WAYS, X_WAYS, rows, sum_cols), bf16),
            pltpu.VMEM((CHUNKS, X_WAYS, rows, sum_cols), bf16),
            pltpu.VMEM((CHUNKS, X_WAYS - 1, rows, sum_cols), bf16),
            dma((CHUNKS, 8)),
            dma((CHUNKS, 8)),
            pltpu.VMEM((shard, slots), bf16),
            pltpu.VMEM((shard, slots), bf16),
            pltpu.VMEM((count, cores, Z_WAYS, X_WAYS, rows, cols), bf16),
            pltpu.VMEM((slots, shard), jnp.float32),
            pltpu.VMEM((blocks, cores, rows // 2, width), bf16),
            pltpu.VMEM((Y_WAYS, PAIR, cores, rows // 2, width), bf16),
            pltpu.VMEM((Y_WAYS, PAIR, cores, rows // 2, width), bf16),
            dma((count, 6)),
            dma((count, 6)),
            dma((blocks * cores,)),
            dma((Y_WAYS, PAIR, cores)),
            dma((Y_WAYS - 1,)),
            dma((Y_WAYS,)),
        ],
        compiler_params=pltpu.CompilerParams(
            collective_id=0, has_side_effects=True, vmem_limit_bytes=59 << 20
        ),
    )(packed, w_gate, w_up, w_down, weight, low, high)


def body(tokens, grad_out, expert_ids, route_weights, w_gate, w_up, w_down):
    experts = lax.axis_size("expert")
    groups = lax.axis_size("dp")
    tok_rows = tokens.shape[0]
    capacity = tok_rows // 2
    expert_index = lax.axis_index("expert")
    inv_root = 1.0 / math.sqrt(tok_rows * groups)
    gate_shard, up_shard, down_shard = w_gate[0], w_up[0], w_down[0].T

    names = jnp.arange(experts, dtype=jnp.int32)[:, None]
    hit0 = expert_ids[:, 0][None, :] == names
    hit1 = expert_ids[:, 1][None, :] == names
    hit = (hit0 | hit1).astype(jnp.bfloat16)
    index = jnp.arange(tok_rows, dtype=jnp.int32)
    before = (index[:, None] < index[None, :]).astype(jnp.bfloat16)
    rank = jnp.dot(hit, before, preferred_element_type=jnp.float32)
    rank = jnp.where(hit > 0, rank, -1.0).astype(jnp.int32)
    chosen = rank[:, None, :] == jnp.arange(capacity, dtype=jnp.int32)[None, :, None]
    pick = chosen.astype(jnp.bfloat16)

    def place(first):
        by_row = rank.reshape(PAIR, Y_WAYS, tok_rows).transpose(2, 1, 0).reshape(tok_rows, experts)
        part = by_row[:, :, None] == jnp.arange(first, first + capacity // 2, dtype=jnp.int32)
        return part.astype(jnp.bfloat16).reshape(tok_rows, experts * capacity // 2)

    weight_of = jnp.where(hit0, route_weights[:, 0][None, :], 0.0) + jnp.where(
        hit1, route_weights[:, 1][None, :], 0.0
    )
    own_rank = lax.dynamic_slice_in_dim(rank, expert_index, 1)
    own_weight_of = lax.dynamic_slice_in_dim(weight_of, expert_index, 1)
    own_weight = jnp.sum(
        jnp.where(
            own_rank == jnp.arange(capacity, dtype=jnp.int32)[:, None], own_weight_of, 0.0
        ),
        axis=1,
    )

    packed = dispatched(pick, tokens, grad_out)
    grad_g, grad_u, grad_d, grad_tokens = expert_rows(
        inv_root, packed, gate_shard, up_shard, down_shard, own_weight[:, None],
        place(0), place(capacity // 2),
    )
    return (grad_tokens, grad_g[None], grad_u[None], grad_d.T[None])


def solution(mesh):
    in_specs = (
        P("dp", "expert"),
        P("dp", "expert"),
        P("dp", None),
        P("dp", None),
        P("expert", "dp", None),
        P("expert", "dp", None),
        P("expert", None, "dp"),
    )
    out_specs = (
        P("dp", "expert"),
        P("expert", "dp", None),
        P("expert", "dp", None),
        P("expert", None, "dp"),
    )
    return jax.shard_map(body, mesh=mesh, in_specs=in_specs, out_specs=out_specs, check_vma=False)
```
